128 devices in a mesh: cuts: 4 (over z), tile: 32 (over y, x, core).
Axes of the slice: x: 4, y: 4, z: 4, core: 2. Of those that a mesh axis runs over, the one named last changes fastest.
Arguments:
- start_states: float32 [4, 3, 512, 2048], P('cuts', None, 'tile'), may hold values from -6 to 6
Outputs:
- next_states: float32 [4, 3, 512, 2048], P('cuts', None, 'tile')
The draws below stay inside these ranges and needn't reach their ends.
All inputs are finite; a program needn't handle non-finite values.
Results may differ from the reference program's by a relative error of at most 0.0001.
Values sent between devices are 32-bit elements; how exact they have to be, the bound alone decides.
No kernel may reach another device: no remote copies, remote signals or barrier semaphores. Data moves between devices by JAX's collectives and lax.ppermute only.
A program may use at most 128 MiB of HBM per device.

```python
import jax
import jax.numpy as jnp
from jax import lax

NX = 2048
STEPS = 3
SLICES = 4
NY = 512
N_CUTS = 4


def level_of(stream_key, extent, shards, smallest, largest):
    gain = 1.0
    for axis_at, shards_of in shards:
        steps = jax.random.uniform(jax.random.fold_in(jax.random.fold_in(stream_key, 6), axis_at), (shards_of,), jnp.float32, smallest / len(shards), largest / len(shards))
        gain = gain * jnp.repeat(jnp.exp(steps), extent[axis_at] // shards_of).reshape((-1,) + (1,) * (len(extent) - 1 - axis_at))
    return gain


def centred(stream_key, extent, spread, limit, shards=(), dtype=jnp.bfloat16):
    result = jax.random.normal(stream_key, extent, jnp.float32) * spread
    if len(shards) > 0:
        result = level_of(stream_key, extent, shards, -0.22, 0.18) * result
    return jnp.clip(result, min=-limit, max=limit).astype(dtype)


def setup_inputs(seed: int = 0) -> dict:
    key_of = jax.random.split(jax.random.key(seed), 2)
    start_states = centred(key_of[0], (SLICES, 3, NY, NX), 1.0, 6.0, ((0, 4), (2, 32)), jnp.float32)
    return dict(start_states=start_states)


FINE_SPACING = 0.05
COARSE_SPACING = 0.1
FINE_STEP = 0.015
COARSE_STEP = 0.045

def depth_profile(columns, stride, length):
    centers = (jnp.arange(columns).astype(jnp.float32) + 0.5) * stride
    return 0.9 + 0.3 * jnp.sin(6.0 * jnp.pi * centers / length)

def along_x(values, spacing):
    padded = jnp.pad(values, [(0, 0)] * (values.ndim - 1) + [(1, 1)])
    return (padded[..., 2:] - padded[..., :-2]) / (2.0 * spacing)

def along_y(values, spacing):
    padded = jnp.pad(values, [(0, 0)] * (values.ndim - 2) + [(1, 1), (0, 0)])
    return (padded[..., 2:, :] - padded[..., :-2, :]) / (2.0 * spacing)

def second_y(values):
    padded = jnp.pad(values, [(0, 0)] * (values.ndim - 2) + [(1, 1), (0, 0)])
    return padded[..., 2:, :] - 2.0 * values + padded[..., :-2, :]

def solve_lines(forcing, seabed, spacing):
    columns = forcing.shape[-1]
    coupling = seabed * seabed / (3.0 * spacing * spacing)
    below_diag = (-coupling).at[0].set(0.0)
    above_diag = (-coupling).at[columns - 1].set(0.0)
    middle = 1.0 + 2.0 * coupling
    stacked_lines = forcing.reshape(-1, columns).T
    solved = lax.linalg.tridiagonal_solve(below_diag, middle, above_diag, stacked_lines)
    return solved.T.reshape(forcing.shape)

def wave_step(fields, seabed, spacing, time_step, inside):
    height = fields[..., 0, :, :]
    flux_x = fields[..., 1, :, :]
    flux_y = fields[..., 2, :, :]
    height_new = (height - time_step * (along_x(flux_x, spacing) + along_y(flux_y, spacing))) * inside
    forcing = jnp.stack([flux_x - time_step * seabed * along_x(height_new, spacing), flux_y - time_step * seabed * along_y(height_new, spacing)], axis=-3)
    trial_flux = solve_lines(forcing, seabed, spacing) * inside
    dispersion = seabed * seabed / 3.0
    weight = dispersion / (spacing * spacing + 4.0 * dispersion)
    fluxes = fields[..., 1:, :, :]
    fluxes_new = (trial_flux + weight * second_y(trial_flux - fluxes)) * inside
    return jnp.concatenate([height_new[..., None, :, :], fluxes_new], axis=-3)

def restrict(fields):
    shape_list = list(fields.shape)
    row_count = shape_list[-2]
    columns = shape_list[-1]
    blocks = fields.reshape(shape_list[:-2] + [row_count // 2, 2, columns // 2, 2])
    return 0.25 * jnp.sum(blocks, axis=(-3, -1))

def prolong(coarse):
    return jnp.repeat(jnp.repeat(coarse, 2, axis=-2), 2, axis=-1)

def reference(start_states):
    columns = start_states.shape[-1]
    fine_depth = depth_profile(columns, 1.0, columns)
    coarse_depth = depth_profile(columns // 2, 2.0, columns)
    fields = start_states
    for substep in range(STEPS):
        fields = wave_step(fields, fine_depth, FINE_SPACING, FINE_STEP, 1.0)
    fine_end = fields
    restricted_start = restrict(start_states)
    restricted_end = restrict(fine_end)
    previous = wave_step(restricted_start, coarse_depth, COARSE_SPACING, COARSE_STEP, 1.0)
    current = restricted_start[0]
    outputs = []
    for slice_index in range(N_CUTS):
        coarse_new = wave_step(current, coarse_depth, COARSE_SPACING, COARSE_STEP, 1.0) - previous[slice_index]
        outputs.append(prolong(coarse_new) + fine_end[slice_index])
        current = coarse_new + restricted_end[slice_index]
    return jnp.stack(outputs)
```

```python
import jax
import jax.numpy as jnp
import ml_dtypes
import numpy as np
from jax import lax
from jax.experimental import pallas as pl
from jax.experimental.pallas import tpu as pltpu
from jax.sharding import PartitionSpec as P

STEPS = 3
FINE_SPACING = 0.05
COARSE_SPACING = 0.1
FINE_STEP = 0.015
COARSE_STEP = 0.045

NX = 2048
ROWS = 16
UNKNOWNS = 512
BLOCKS = 4
LANES = 128
HALO_ROWS = 32
COARSE_HALO = 9
VMEM_LIMIT = 48 * 1024 * 1024


def halves(values):
    high = values.astype(np.float32).astype(ml_dtypes.bfloat16)
    low = (values - high.astype(np.float64)).astype(np.float32).astype(ml_dtypes.bfloat16)
    return high, low


def shifted(values):
    return np.concatenate([[0.0], values[:-1]])


def eliminated(lower, middle, upper):
    lower_e, lower_o = lower[0::2], lower[1::2]
    middle_e, middle_o = middle[0::2], middle[1::2]
    upper_e, upper_o = upper[0::2], upper[1::2]
    middle_n = np.append(middle_e[1:], 1.0)
    lower_n = np.append(lower_e[1:], 0.0)
    upper_n = np.append(upper_e[1:], 0.0)
    alpha = -lower_o / middle_e
    gamma = -upper_o / middle_n
    reduced = (alpha * lower_e, middle_o + alpha * upper_e + gamma * lower_n, gamma * upper_n)
    return alpha, gamma, reduced


def operator_tables(phases, columns, spacing, time_step):
    stride = NX // columns
    centers = (np.arange(columns) + 0.5) * stride
    depth = 0.9 + 0.3 * np.sin(6.0 * np.pi * centers / NX)
    beta = depth * depth / 3.0
    coupling = beta / (spacing * spacing)
    lower = -coupling.copy()
    lower[0] = 0.0
    upper = -coupling.copy()
    upper[-1] = 0.0
    middle = 1.0 + 2.0 * coupling
    slope = time_step * depth / (2.0 * spacing)
    weight = beta / (spacing * spacing + 4.0 * beta)
    rows = {}
    for p in range(phases):
        rows["slope", p] = slope[p::phases]
        rows["weight", p] = weight[p::phases]
    alpha, gamma, first = eliminated(lower, middle, upper)
    if phases == 4:
        alpha2, gamma2, last = eliminated(*first)
        a1, a3, g1, g3 = alpha[0::2], alpha[1::2], gamma[0::2], gamma[1::2]
        rows["s0"] = alpha2 * a1
        rows["s1"] = alpha2
        rows["s2"] = a3 + alpha2 * g1
        rows["n1"] = shifted(gamma2)
        rows["n0"] = shifted(gamma2) * a1 + shifted(g3)
        rows["n2"] = shifted(gamma2) * g1
        l1, m1, u1 = (v[0::2] for v in first)
        rows["b1"] = 1.0 / m1
        rows["b0"] = a1 / m1
        rows["b2"] = g1 / m1
        rows["bp"] = -l1 / m1
        rows["b3"] = -u1 / m1
        rows["c0"] = 1.0 / middle[0::4]
        rows["cp"] = -lower[0::4] / middle[0::4]
        rows["c1"] = -upper[0::4] / middle[0::4]
        rows["d2"] = 1.0 / middle[2::4]
        rows["d1"] = -lower[2::4] / middle[2::4]
        rows["d3"] = -upper[2::4] / middle[2::4]
    else:
        last = first
        rows["s0"] = alpha
        rows["n0"] = shifted(gamma)
        rows["c0"] = 1.0 / middle[0::2]
        rows["cp"] = -lower[0::2] / middle[0::2]
        rows["c1"] = -upper[0::2] / middle[0::2]
    low, mid, up = last
    matrix = np.diag(mid) + np.diag(low[1:], -1) + np.diag(up[:-1], 1)
    inverse = np.linalg.inv(matrix)
    names = {name: i for i, name in enumerate(rows)}
    table = np.stack(list(rows.values())).reshape(-1, LANES).astype(np.float32)
    return names, table, np.stack(halves(inverse.T))


FINE_NAMES, FINE_TABLE, FINE_INVERSE = operator_tables(4, NX, FINE_SPACING, FINE_STEP)
COARSE_NAMES, COARSE_TABLE, COARSE_INVERSE = operator_tables(2, NX // 2, COARSE_SPACING, COARSE_STEP)


def phase_matrix():
    matrix = np.zeros((512, 512), np.float32)
    j = np.arange(512)
    matrix[j, (j % 4) * LANES + j // 4] = 1.0
    return matrix


PHASES = phase_matrix().astype(ml_dtypes.bfloat16)
NATURAL = phase_matrix().T.copy().astype(ml_dtypes.bfloat16)


def spread_matrix():
    matrix = np.zeros((256, 512), np.float32)
    c = np.arange(512)
    coarse = c // 2
    matrix[(coarse % 2) * LANES + coarse // 2, c] = 1.0
    return matrix


SPREAD = spread_matrix().astype(ml_dtypes.bfloat16)


def split(values):
    high = values.astype(jnp.bfloat16)
    low = (values - high.astype(jnp.float32)).astype(jnp.bfloat16)
    return high, low


def dot(a, b):
    return jnp.dot(a, b, preferred_element_type=jnp.float32)


def placed(values, matrix):
    count = values.shape[0]
    high, low = split(values)
    both = dot(jnp.concatenate([high, low], axis=0), matrix)
    return both[:count] + both[count:]


def lane_index(rows):
    return lax.broadcasted_iota(jnp.int32, (rows, LANES), 1)


def following(tiles):
    lane = lane_index(tiles[0].shape[0])
    rolled = [pltpu.roll(t, LANES - 1, 1) for t in tiles] + [jnp.zeros_like(tiles[0])]
    return [jnp.where(lane == LANES - 1, rolled[a + 1], rolled[a]) for a in range(BLOCKS)]


def preceding(tiles):
    lane = lane_index(tiles[0].shape[0])
    rolled = [jnp.zeros_like(tiles[0])] + [pltpu.roll(t, 1, 1) for t in tiles]
    return [jnp.where(lane == 0, rolled[a], rolled[a + 1]) for a in range(BLOCKS)]


def inside(first, count, total):
    row = lax.broadcasted_iota(jnp.int32, (count, LANES), 0) + first
    return jnp.where((row >= 0) & (row < total), 1.0, 0.0).astype(jnp.float32)


def wave_step(phases, names, table, inverse, ratio, height, height_new, flux, diff, windows, origin, total):
    (h0, hn), (d0, dn), (o0, on) = windows
    last = phases - 1

    def coef(name, a):
        i = names[name] * BLOCKS + a
        return table[i : i + 1, :]

    mask = inside(origin + h0, hn, total)
    rows = pl.ds(h0, hn)
    before = preceding([flux[0, last, a, rows, :] for a in range(BLOCKS)])
    after = following([flux[0, 0, a, rows, :] for a in range(BLOCKS)])
    for p in range(phases):
        for a in range(BLOCKS):
            right = after[a] if p == last else flux[0, p + 1, a, rows, :]
            left = before[a] if p == 0 else flux[0, p - 1, a, rows, :]
            down = flux[1, p, a, pl.ds(h0 + 1, hn), :]
            upper = flux[1, p, a, pl.ds(h0 - 1, hn), :]
            change = (right - left) + (down - upper)
            height_new[p, a, rows, :] = (height[p, a, rows, :] - ratio * change) * mask

    rows = pl.ds(d0, dn)
    mask = inside(origin + d0, dn, total)
    before = preceding([height_new[last, a, rows, :] for a in range(BLOCKS)])
    after = following([height_new[0, a, rows, :] for a in range(BLOCKS)])
    reduced = []
    for i in range(2):
        own, passed = [], []
        for a in range(BLOCKS):
            force = []
            for p in range(phases):
                if i == 0:
                    right = after[a] if p == last else height_new[p + 1, a, rows, :]
                    left = before[a] if p == 0 else height_new[p - 1, a, rows, :]
                    value = flux[0, p, a, rows, :] - coef(("slope", p), a) * (right - left)
                else:
                    down = height_new[p, a, pl.ds(d0 + 1, dn), :]
                    upper = height_new[p, a, pl.ds(d0 - 1, dn), :]
                    value = (flux[1, p, a, rows, :] - coef(("slope", p), a) * (down - upper)) * mask
                if p < last:
                    diff[i, p, a, rows, :] = value
                force.append(value)
            kept = force[last] + coef("s0", a) * force[0]
            sent = coef("n0", a) * force[0]
            if phases == 4:
                kept = kept + coef("s1", a) * force[1] + coef("s2", a) * force[2]
                sent = sent + coef("n1", a) * force[1] + coef("n2", a) * force[2]
            own.append(kept)
            passed.append(sent)
        arrived = following(passed)
        reduced.append(jnp.concatenate([own[a] + arrived[a] for a in range(BLOCKS)], axis=1))
    high, low = split(jnp.concatenate(reduced, axis=0))
    both = dot(jnp.concatenate([high, low], axis=0), inverse[0])
    solved = both[: 2 * dn] + both[2 * dn :] + dot(high, inverse[1])

    for i in range(2):
        ends = [solved[i * dn : (i + 1) * dn, a * LANES : (a + 1) * LANES] for a in range(BLOCKS)]
        before = preceding(ends)
        for a in range(BLOCKS):
            end, prior = ends[a], before[a]
            f0 = diff[i, 0, a, rows, :]
            if phases == 4:
                f1 = diff[i, 1, a, rows, :]
                f2 = diff[i, 2, a, rows, :]
                x1 = (
                    coef("b1", a) * f1
                    + coef("b0", a) * f0
                    + coef("b2", a) * f2
                    + coef("bp", a) * prior
                    + coef("b3", a) * end
                )
                x0 = coef("c0", a) * f0 + coef("cp", a) * prior + coef("c1", a) * x1
                x2 = coef("d2", a) * f2 + coef("d1", a) * x1 + coef("d3", a) * end
                trial = [x0, x1, x2, end]
            else:
                trial = [coef("c0", a) * f0 + coef("cp", a) * prior + coef("c1", a) * end, end]
            for p in range(phases):
                diff[i, p, a, rows, :] = trial[p] - flux[i, p, a, rows, :]

    mask = inside(origin + o0, on, total)
    rows = pl.ds(o0, on)
    for i in range(2):
        for p in range(phases):
            for a in range(BLOCKS):
                middle = diff[i, p, a, rows, :]
                down = diff[i, p, a, pl.ds(o0 + 1, on), :]
                upper = diff[i, p, a, pl.ds(o0 - 1, on), :]
                bend = coef(("weight", p), a) * (down + upper - 2.0 * middle)
                flux[i, p, a, rows, :] = (flux[i, p, a, rows, :] + middle + bend) * mask


FINE_RATIO = FINE_STEP / (2.0 * FINE_SPACING)
COARSE_RATIO = COARSE_STEP / (2.0 * COARSE_SPACING)


def pack_kernel(x, to_next, to_previous):
    for s in range(16):
        cols = slice(s * LANES, (s + 1) * LANES)
        base = s * HALO_ROWS
        for c, (start, count) in enumerate(((0, 10), (10, 11), (21, 11))):
            to_next[base + start : base + start + count, :] = x[c, ROWS - count : ROWS, cols]
            to_previous[base + start : base + start + count, :] = x[c, 0:count, cols]


def own_kernel(x, matrix, out):
    parts = []
    for a in range(BLOCKS):
        for c in range(3):
            parts.append(x[c, :, a * 512 : (a + 1) * 512])
    phased = placed(jnp.concatenate(parts, axis=0), matrix[...])
    for a in range(BLOCKS):
        for c in range(3):
            base = (a * 3 + c) * ROWS
            for p in range(4):
                out[c, p, a] = phased[base : base + ROWS, p * LANES : (p + 1) * LANES]


def fine_kernel(
    own, above, below, matrix, fine_inverse, coarse_inverse, fine_table, coarse_table,
    fine_end, u_own, u_next, u_previous, propagated,
    height, height_new, flux, diff, c_height, c_height_new, c_flux, c_diff,
):
    tile = lax.axis_index("tile")
    cut = lax.axis_index("cuts")
    tiles = lax.axis_size("tile")
    parts = []
    for a in range(BLOCKS):
        for halo in (above, below):
            parts.append(
                jnp.concatenate(
                    [halo[(4 * a + s) * HALO_ROWS : (4 * a + s + 1) * HALO_ROWS, :] for s in range(4)],
                    axis=1,
                )
            )
    phased = placed(jnp.concatenate(parts, axis=0), matrix[...])

    def field(c, p, a):
        return height.at[p, a] if c == 0 else flux.at[c - 1, p, a]

    for a in range(BLOCKS):
        for p in range(4):
            lanes = slice(p * LANES, (p + 1) * LANES)
            top = a * 2 * HALO_ROWS
            low = top + HALO_ROWS
            for c, (start, count) in enumerate(((0, 10), (10, 11), (21, 11))):
                to = field(c, p, a)
                to[16 - count : 16, :] = phased[top + start : top + start + count, lanes]
                to[16:32, :] = own[c, p, a]
                to[32 : 32 + count, :] = phased[low + start : low + start + count, lanes]

    def restricted(ref, p, a):
        total = None
        for q in (2 * p, 2 * p + 1):
            for r in (8, 9):
                part = ref(q, a)[pl.ds(r, 16, stride=2), :]
                total = part if total is None else total + part
        return 0.25 * total

    for p in range(2):
        for a in range(BLOCKS):
            c_height[p, a, 8:24, :] = restricted(lambda q, b: height.at[q, b], p, a)
            for i in range(2):
                c_flux[i, p, a, 8:24, :] = restricted(lambda q, b: flux.at[i, q, b], p, a)

    wave_step(
        2, COARSE_NAMES, coarse_table, coarse_inverse, COARSE_RATIO, c_height, c_height_new, c_flux, c_diff,
        ((8, 16), (8, 16), (8, 16)), tile * (ROWS // 2) - 12, tiles * (ROWS // 2),
    )

    origin = tile * ROWS - 16
    total = tiles * ROWS
    arguments = (4, FINE_NAMES, fine_table, fine_inverse, FINE_RATIO)
    wave_step(*arguments, height, height_new, flux, diff, ((4, 40), (4, 40), (8, 32)), origin, total)
    wave_step(*arguments, height_new, height, flux, diff, ((8, 32), (8, 32), (8, 32)), origin, total)
    wave_step(*arguments, height, height_new, flux, diff, ((12, 24), (12, 24), (12, 24)), origin, total)

    for p in range(4):
        for a in range(BLOCKS):
            fine_end[0, p, a] = height_new[p, a, 16:32, :]
            for i in range(2):
                fine_end[i + 1, p, a] = flux[i, p, a, 16:32, :]

    later = jnp.where(cut > 0, 1.0, 0.0).astype(jnp.float32)
    for c in range(3):
        for p in range(2):
            for a in range(BLOCKS):
                if c == 0:
                    end = restricted(lambda q, b: height_new.at[q, b], p, a)
                    step = c_height_new[p, a, 8:24, :]
                else:
                    end = restricted(lambda q, b: flux.at[c - 1, q, b], p, a)
                    step = c_flux[c - 1, p, a, 8:24, :]
                step = later * step
                propagated[c, p, a] = step[4:12]
                u = end - step
                c_diff[0, p, a, 8:24, :] = u
                u_own[c, p, a] = u[4:12]
                base = ((c * 2 + p) * BLOCKS + a) * COARSE_HALO
                u_next[base : base + COARSE_HALO, :] = c_diff[0, p, a, 11:20, :]
                u_previous[base : base + COARSE_HALO, :] = c_diff[0, p, a, 12:21, :]


def natural_kernel(fine_end, matrix, out):
    parts = []
    for a in range(BLOCKS):
        for c in range(3):
            parts.append(jnp.concatenate([fine_end[c, p, a] for p in range(4)], axis=1))
    natural = placed(jnp.concatenate(parts, axis=0), matrix[...])
    for a in range(BLOCKS):
        for c in range(3):
            base = (a * 3 + c) * ROWS
            out[c, :, a * 512 : (a + 1) * 512] = natural[base : base + ROWS]


def coarse_kernel(own, above, below, inverse, table, one, two, three, height, height_new, flux, diff):
    tile = lax.axis_index("tile")
    tiles = lax.axis_size("tile")
    for c in range(3):
        for p in range(2):
            for a in range(BLOCKS):
                to = height.at[p, a] if c == 0 else flux.at[c - 1, p, a]
                base = ((c * 2 + p) * BLOCKS + a) * COARSE_HALO
                to[7:16, :] = above[base : base + COARSE_HALO, :]
                to[16:24, :] = own[c, p, a]
                to[24:33, :] = below[base : base + COARSE_HALO, :]
    origin = tile * (ROWS // 2) - 16
    total = tiles * (ROWS // 2)
    arguments = (2, COARSE_NAMES, table, inverse, COARSE_RATIO)

    def keep(out, source):
        for p in range(2):
            for a in range(BLOCKS):
                out[0, p, a] = source[p, a, 16:24, :]
                for i in range(2):
                    out[i + 1, p, a] = flux[i, p, a, 16:24, :]

    wave_step(*arguments, height, height_new, flux, diff, ((8, 24), (8, 24), (8, 24)), origin, total)
    keep(one, height_new)
    wave_step(*arguments, height_new, height, flux, diff, ((8, 24), (12, 16), (12, 16)), origin, total)
    keep(two, height)
    wave_step(*arguments, height, height_new, flux, diff, ((12, 16), (12, 16), (16, 8)), origin, total)
    keep(three, height_new)


def final_kernel(fine_end, propagated, one, two, three, matrix, out, rows):
    parts = []
    for a in range(BLOCKS):
        for c in range(3):
            pair = []
            for p in range(2):
                pair.append(one[c, p, a] + two[c, p, a] + three[c, p, a] - propagated[c, p, a])
            parts.append(jnp.concatenate(pair, axis=1))
    spread = placed(jnp.concatenate(parts, axis=0), matrix[...])
    for a in range(BLOCKS):
        for c in range(3):
            base = (a * 3 + c) * 8
            for s in range(4):
                value = spread[base : base + 8, s * LANES : (s + 1) * LANES]
                rows[c, a * 4 + s, pl.ds(0, 8, stride=2), :] = value
                rows[c, a * 4 + s, pl.ds(1, 8, stride=2), :] = value
    for c in range(3):
        for s in range(16):
            cols = slice(s * LANES, (s + 1) * LANES)
            out[c, :, cols] = fine_end[c, :, cols] + rows[c, s]


def f32(*shape):
    return jax.ShapeDtypeStruct(shape, jnp.float32)


def scratch(*shape):
    return pltpu.VMEM(shape, jnp.float32)


def call(kernel, outs, scratches=(), name=None):
    return pl.pallas_call(
        kernel,
        out_shape=outs,
        scratch_shapes=scratches,
        name=name,
        compiler_params=pltpu.CompilerParams(vmem_limit_bytes=VMEM_LIMIT),
    )


def per_device(start_states):
    x = start_states[0]
    tiles = lax.axis_size("tile")
    slices = lax.axis_size("cuts")
    forward = [(i, i + 1) for i in range(tiles - 1)]
    backward = [(i + 1, i) for i in range(tiles - 1)]

    halo = f32(16 * HALO_ROWS, LANES)
    to_next, to_previous = call(pack_kernel, [halo, halo], name="pack")(x)
    above = lax.ppermute(to_next, "tile", forward)
    below = lax.ppermute(to_previous, "tile", backward)
    own = call(own_kernel, f32(3, 4, BLOCKS, ROWS, LANES), name="phases")(x, PHASES)

    coarse = f32(3, 2, BLOCKS, 8, LANES)
    coarse_halo = f32(3 * 2 * BLOCKS * COARSE_HALO, LANES)
    fine_end, u_own, u_next, u_previous, propagated = call(
        fine_kernel,
        [f32(3, 4, BLOCKS, ROWS, LANES), coarse, coarse_halo, coarse_halo, coarse],
        [
            scratch(4, BLOCKS, 48, LANES),
            scratch(4, BLOCKS, 48, LANES),
            scratch(2, 4, BLOCKS, 48, LANES),
            scratch(2, 4, BLOCKS, 48, LANES),
            scratch(2, BLOCKS, 32, LANES),
            scratch(2, BLOCKS, 32, LANES),
            scratch(2, 2, BLOCKS, 32, LANES),
            scratch(2, 2, BLOCKS, 32, LANES),
        ],
        name="fine",
    )(own, above, below, PHASES, FINE_INVERSE, COARSE_INVERSE, FINE_TABLE, COARSE_TABLE)

    u_above = lax.ppermute(u_next, "tile", forward)
    u_below = lax.ppermute(u_previous, "tile", backward)
    natural = call(natural_kernel, f32(3, ROWS, NX), name="natural")(fine_end, NATURAL)

    powers = call(
        coarse_kernel,
        [coarse, coarse, coarse],
        [
            scratch(2, BLOCKS, 48, LANES),
            scratch(2, BLOCKS, 48, LANES),
            scratch(2, 2, BLOCKS, 48, LANES),
            scratch(2, 2, BLOCKS, 48, LANES),
        ],
        name="coarse",
    )(u_own, u_above, u_below, COARSE_INVERSE, COARSE_TABLE)
    arrived = [
        lax.ppermute(power, "cuts", [(i, i + m) for i in range(slices - m)])
        for m, power in enumerate(powers, 1)
    ]
    out = call(final_kernel, f32(3, ROWS, NX), [scratch(3, 16, ROWS, LANES)], name="final")(
        natural, propagated, *arrived, SPREAD
    )
    return out[None]


def solution(mesh):
    spec = P("cuts", None, "tile", None)
    return jax.shard_map(per_device, mesh=mesh, in_specs=(spec,), out_specs=spec, check_vma=False)
```

```python
import jax
import jax.numpy as jnp
import ml_dtypes
import numpy as np
from jax import lax
from jax.experimental import pallas as pl
from jax.experimental.pallas import tpu as pltpu
from jax.sharding import PartitionSpec as P

STEPS = 3
FINE_SPACING = 0.05
COARSE_SPACING = 0.1
FINE_STEP = 0.015
COARSE_STEP = 0.045

NX = 2048
ROWS = 16
UNKNOWNS = 512
BLOCKS = 4
LANES = 128
HALO_ROWS = 32
COARSE_HALO = 9
VMEM_LIMIT = 48 * 1024 * 1024


def halves(values):
    high = values.astype(np.float32).astype(ml_dtypes.bfloat16)
    low = (values - high.astype(np.float64)).astype(np.float32).astype(ml_dtypes.bfloat16)
    return high, low


def shifted(values):
    return np.concatenate([[0.0], values[:-1]])


def eliminated(lower, middle, upper):
    lower_e, lower_o = lower[0::2], lower[1::2]
    middle_e, middle_o = middle[0::2], middle[1::2]
    upper_e, upper_o = upper[0::2], upper[1::2]
    middle_n = np.append(middle_e[1:], 1.0)
    lower_n = np.append(lower_e[1:], 0.0)
    upper_n = np.append(upper_e[1:], 0.0)
    alpha = -lower_o / middle_e
    gamma = -upper_o / middle_n
    reduced = (alpha * lower_e, middle_o + alpha * upper_e + gamma * lower_n, gamma * upper_n)
    return alpha, gamma, reduced


def operator_tables(phases, columns, spacing, time_step):
    stride = NX // columns
    centers = (np.arange(columns) + 0.5) * stride
    depth = 0.9 + 0.3 * np.sin(6.0 * np.pi * centers / NX)
    beta = depth * depth / 3.0
    coupling = beta / (spacing * spacing)
    lower = -coupling.copy()
    lower[0] = 0.0
    upper = -coupling.copy()
    upper[-1] = 0.0
    middle = 1.0 + 2.0 * coupling
    slope = time_step * depth / (2.0 * spacing)
    weight = beta / (spacing * spacing + 4.0 * beta)
    rows = {}
    for p in range(phases):
        rows["slope", p] = slope[p::phases]
        rows["weight", p] = weight[p::phases]
    alpha, gamma, first = eliminated(lower, middle, upper)
    if phases == 4:
        alpha2, gamma2, last = eliminated(*first)
        a1, a3, g1, g3 = alpha[0::2], alpha[1::2], gamma[0::2], gamma[1::2]
        rows["s0"] = alpha2 * a1
        rows["s1"] = alpha2
        rows["s2"] = a3 + alpha2 * g1
        rows["n1"] = shifted(gamma2)
        rows["n0"] = shifted(gamma2) * a1 + shifted(g3)
        rows["n2"] = shifted(gamma2) * g1
        l1, m1, u1 = (v[0::2] for v in first)
        rows["b1"] = 1.0 / m1
        rows["b0"] = a1 / m1
        rows["b2"] = g1 / m1
        rows["bp"] = -l1 / m1
        rows["b3"] = -u1 / m1
        rows["c0"] = 1.0 / middle[0::4]
        rows["cp"] = -lower[0::4] / middle[0::4]
        rows["c1"] = -upper[0::4] / middle[0::4]
        rows["d2"] = 1.0 / middle[2::4]
        rows["d1"] = -lower[2::4] / middle[2::4]
        rows["d3"] = -upper[2::4] / middle[2::4]
    else:
        last = first
        rows["s0"] = alpha
        rows["n0"] = shifted(gamma)
        rows["c0"] = 1.0 / middle[0::2]
        rows["cp"] = -lower[0::2] / middle[0::2]
        rows["c1"] = -upper[0::2] / middle[0::2]
    low, mid, up = last
    matrix = np.diag(mid) + np.diag(low[1:], -1) + np.diag(up[:-1], 1)
    inverse = np.linalg.inv(matrix)
    names = {name: i for i, name in enumerate(rows)}
    table = np.stack(list(rows.values())).reshape(-1, LANES).astype(np.float32)
    return names, table, np.stack(halves(inverse.T))


FINE_NAMES, FINE_TABLE, FINE_INVERSE = operator_tables(4, NX, FINE_SPACING, FINE_STEP)
COARSE_NAMES, COARSE_TABLE, COARSE_INVERSE = operator_tables(2, NX // 2, COARSE_SPACING, COARSE_STEP)


def phase_matrix():
    matrix = np.zeros((512, 512), np.float32)
    j = np.arange(512)
    matrix[j, (j % 4) * LANES + j // 4] = 1.0
    return matrix


PHASES = phase_matrix().astype(ml_dtypes.bfloat16)
NATURAL = phase_matrix().T.copy().astype(ml_dtypes.bfloat16)


def spread_matrix():
    matrix = np.zeros((256, 512), np.float32)
    c = np.arange(512)
    coarse = c // 2
    matrix[(coarse % 2) * LANES + coarse // 2, c] = 1.0
    return matrix


SPREAD = spread_matrix().astype(ml_dtypes.bfloat16)


def split(values):
    high = values.astype(jnp.bfloat16)
    low = (values - high.astype(jnp.float32)).astype(jnp.bfloat16)
    return high, low


def dot(a, b):
    return jnp.dot(a, b, preferred_element_type=jnp.float32)


def placed(values, matrix):
    count = values.shape[0]
    high, low = split(values)
    both = dot(jnp.concatenate([high, low], axis=0), matrix)
    return both[:count] + both[count:]


def lane_index(rows):
    return lax.broadcasted_iota(jnp.int32, (rows, LANES), 1)


def following(tiles):
    lane = lane_index(tiles[0].shape[0])
    rolled = [pltpu.roll(t, LANES - 1, 1) for t in tiles] + [jnp.zeros_like(tiles[0])]
    return [jnp.where(lane == LANES - 1, rolled[a + 1], rolled[a]) for a in range(BLOCKS)]


def preceding(tiles):
    lane = lane_index(tiles[0].shape[0])
    rolled = [jnp.zeros_like(tiles[0])] + [pltpu.roll(t, 1, 1) for t in tiles]
    return [jnp.where(lane == 0, rolled[a], rolled[a + 1]) for a in range(BLOCKS)]


def inside(first, count, total):
    row = lax.broadcasted_iota(jnp.int32, (count, LANES), 0) + first
    return jnp.where((row >= 0) & (row < total), 1.0, 0.0).astype(jnp.float32)


def wave_step(phases, names, table, inverse, ratio, height, height_new, flux, diff, windows, origin, total):
    (h0, hn), (d0, dn), (o0, on) = windows
    last = phases - 1

    def coef(name, a):
        i = names[name] * BLOCKS + a
        return table[i : i + 1, :]

    mask = inside(origin + h0, hn, total)
    rows = pl.ds(h0, hn)
    before = preceding([flux[0, last, a, rows, :] for a in range(BLOCKS)])
    after = following([flux[0, 0, a, rows, :] for a in range(BLOCKS)])
    for p in range(phases):
        for a in range(BLOCKS):
            right = after[a] if p == last else flux[0, p + 1, a, rows, :]
            left = before[a] if p == 0 else flux[0, p - 1, a, rows, :]
            down = flux[1, p, a, pl.ds(h0 + 1, hn), :]
            upper = flux[1, p, a, pl.ds(h0 - 1, hn), :]
            change = (right - left) + (down - upper)
            height_new[p, a, rows, :] = (height[p, a, rows, :] - ratio * change) * mask

    rows = pl.ds(d0, dn)
    mask = inside(origin + d0, dn, total)
    before = preceding([height_new[last, a, rows, :] for a in range(BLOCKS)])
    after = following([height_new[0, a, rows, :] for a in range(BLOCKS)])
    reduced = []
    for i in range(2):
        own, passed = [], []
        for a in range(BLOCKS):
            force = []
            for p in range(phases):
                if i == 0:
                    right = after[a] if p == last else height_new[p + 1, a, rows, :]
                    left = before[a] if p == 0 else height_new[p - 1, a, rows, :]
                    value = flux[0, p, a, rows, :] - coef(("slope", p), a) * (right - left)
                else:
                    down = height_new[p, a, pl.ds(d0 + 1, dn), :]
                    upper = height_new[p, a, pl.ds(d0 - 1, dn), :]
                    value = (flux[1, p, a, rows, :] - coef(("slope", p), a) * (down - upper)) * mask
                if p < last:
                    diff[i, p, a, rows, :] = value
                force.append(value)
            kept = force[last] + coef("s0", a) * force[0]
            sent = coef("n0", a) * force[0]
            if phases == 4:
                kept = kept + coef("s1", a) * force[1] + coef("s2", a) * force[2]
                sent = sent + coef("n1", a) * force[1] + coef("n2", a) * force[2]
            own.append(kept)
            passed.append(sent)
        arrived = following(passed)
        reduced.append(jnp.concatenate([own[a] + arrived[a] for a in range(BLOCKS)], axis=1))
    high, low = split(jnp.concatenate(reduced, axis=0))
    both = dot(jnp.concatenate([high, low], axis=0), inverse[0])
    solved = both[: 2 * dn] + both[2 * dn :] + dot(high, inverse[1])

    for i in range(2):
        ends = [solved[i * dn : (i + 1) * dn, a * LANES : (a + 1) * LANES] for a in range(BLOCKS)]
        before = preceding(ends)
        for a in range(BLOCKS):
            end, prior = ends[a], before[a]
            f0 = diff[i, 0, a, rows, :]
            if phases == 4:
                f1 = diff[i, 1, a, rows, :]
                f2 = diff[i, 2, a, rows, :]
                x1 = (
                    coef("b1", a) * f1
                    + coef("b0", a) * f0
                    + coef("b2", a) * f2
                    + coef("bp", a) * prior
                    + coef("b3", a) * end
                )
                x0 = coef("c0", a) * f0 + coef("cp", a) * prior + coef("c1", a) * x1
                x2 = coef("d2", a) * f2 + coef("d1", a) * x1 + coef("d3", a) * end
                trial = [x0, x1, x2, end]
            else:
                trial = [coef("c0", a) * f0 + coef("cp", a) * prior + coef("c1", a) * end, end]
            for p in range(phases):
                diff[i, p, a, rows, :] = trial[p] - flux[i, p, a, rows, :]

    mask = inside(origin + o0, on, total)
    rows = pl.ds(o0, on)
    for i in range(2):
        for p in range(phases):
            for a in range(BLOCKS):
                middle = diff[i, p, a, rows, :]
                down = diff[i, p, a, pl.ds(o0 + 1, on), :]
                upper = diff[i, p, a, pl.ds(o0 - 1, on), :]
                bend = coef(("weight", p), a) * (down + upper - 2.0 * middle)
                flux[i, p, a, rows, :] = (flux[i, p, a, rows, :] + middle + bend) * mask


FINE_RATIO = FINE_STEP / (2.0 * FINE_SPACING)
COARSE_RATIO = COARSE_STEP / (2.0 * COARSE_SPACING)


def on_odd():
    return lax.rem(lax.axis_index("tile"), 2) == 1


def pack_kernel(source, x, to_far, to_near, sems):
    copies = [pltpu.make_async_copy(source.at[c], x.at[c], sems.at[c]) for c in range(3)]
    for copy in copies:
        copy.start()
    for copy in copies:
        copy.wait()

    def pack(to_next, to_previous):
        for s in range(16):
            cols = slice(s * LANES, (s + 1) * LANES)
            base = s * HALO_ROWS
            for c, (start, count) in enumerate(((0, 10), (10, 11), (21, 11))):
                to_next[base + start : base + start + count, :] = x[c, ROWS - count : ROWS, cols]
                to_previous[base + start : base + start + count, :] = x[c, 0:count, cols]

    odd = on_odd()
    pl.when(odd)(lambda: pack(to_far, to_near))
    pl.when(jnp.logical_not(odd))(lambda: pack(to_near, to_far))


def own_kernel(x, matrix, inverse, out, inverse_here, sem):
    copy = pltpu.make_async_copy(inverse, inverse_here, sem)
    copy.start()
    parts = []
    for a in range(BLOCKS):
        for c in range(3):
            parts.append(x[c, :, a * 512 : (a + 1) * 512])
    phased = placed(jnp.concatenate(parts, axis=0), matrix[...])
    for a in range(BLOCKS):
        for c in range(3):
            base = (a * 3 + c) * ROWS
            for p in range(4):
                out[c, p, a] = phased[base : base + ROWS, p * LANES : (p + 1) * LANES]
    copy.wait()


def fine_kernel(
    own, far, near, matrix, fine_inverse, coarse_inverse, fine_table, coarse_table,
    fine_end, u_own, u_far, u_near, propagated,
    height, height_new, flux, diff, c_height, c_height_new, c_flux, c_diff,
):
    tile = lax.axis_index("tile")
    cut = lax.axis_index("cuts")
    tiles = lax.axis_size("tile")
    odd = on_odd()
    parts = []
    for a in range(BLOCKS):
        ends = []
        for halo in (far, near):
            ends.append(
                jnp.concatenate(
                    [halo[(4 * a + s) * HALO_ROWS : (4 * a + s + 1) * HALO_ROWS, :] for s in range(4)],
                    axis=1,
                )
            )
        parts += [jnp.where(odd, ends[1], ends[0]), jnp.where(odd, ends[0], ends[1])]
    phased = placed(jnp.concatenate(parts, axis=0), matrix[...])

    def field(c, p, a):
        return height.at[p, a] if c == 0 else flux.at[c - 1, p, a]

    for a in range(BLOCKS):
        for p in range(4):
            lanes = slice(p * LANES, (p + 1) * LANES)
            top = a * 2 * HALO_ROWS
            low = top + HALO_ROWS
            for c, (start, count) in enumerate(((0, 10), (10, 11), (21, 11))):
                to = field(c, p, a)
                to[16 - count : 16, :] = phased[top + start : top + start + count, lanes]
                to[16:32, :] = own[c, p, a]
                to[32 : 32 + count, :] = phased[low + start : low + start + count, lanes]

    def restricted(ref, p, a):
        total = None
        for q in (2 * p, 2 * p + 1):
            for r in (8, 9):
                part = ref(q, a)[pl.ds(r, 16, stride=2), :]
                total = part if total is None else total + part
        return 0.25 * total

    for p in range(2):
        for a in range(BLOCKS):
            c_height[p, a, 8:24, :] = restricted(lambda q, b: height.at[q, b], p, a)
            for i in range(2):
                c_flux[i, p, a, 8:24, :] = restricted(lambda q, b: flux.at[i, q, b], p, a)

    wave_step(
        2, COARSE_NAMES, coarse_table, coarse_inverse, COARSE_RATIO, c_height, c_height_new, c_flux, c_diff,
        ((8, 16), (8, 16), (8, 16)), tile * (ROWS // 2) - 12, tiles * (ROWS // 2),
    )

    origin = tile * ROWS - 16
    total = tiles * ROWS
    arguments = (4, FINE_NAMES, fine_table, fine_inverse, FINE_RATIO)
    wave_step(*arguments, height, height_new, flux, diff, ((4, 40), (4, 40), (8, 32)), origin, total)
    wave_step(*arguments, height_new, height, flux, diff, ((8, 32), (8, 32), (8, 32)), origin, total)
    wave_step(*arguments, height, height_new, flux, diff, ((12, 24), (12, 24), (12, 24)), origin, total)

    for p in range(4):
        for a in range(BLOCKS):
            fine_end[0, p, a] = height_new[p, a, 16:32, :]
            for i in range(2):
                fine_end[i + 1, p, a] = flux[i, p, a, 16:32, :]

    later = jnp.where(cut > 0, 1.0, 0.0).astype(jnp.float32)
    for c in range(3):
        for p in range(2):
            for a in range(BLOCKS):
                if c == 0:
                    end = restricted(lambda q, b: height_new.at[q, b], p, a)
                    step = c_height_new[p, a, 8:24, :]
                else:
                    end = restricted(lambda q, b: flux.at[c - 1, q, b], p, a)
                    step = c_flux[c - 1, p, a, 8:24, :]
                step = later * step
                propagated[c, p, a] = step[4:12]
                u = end - step
                c_diff[0, p, a, 8:24, :] = u
                u_own[c, p, a] = u[4:12]
                base = ((c * 2 + p) * BLOCKS + a) * COARSE_HALO
                to_next = c_diff[0, p, a, 11:20, :]
                to_previous = c_diff[0, p, a, 12:21, :]
                u_far[base : base + COARSE_HALO, :] = jnp.where(odd, to_next, to_previous)
                u_near[base : base + COARSE_HALO, :] = jnp.where(odd, to_previous, to_next)


def natural_kernel(fine_end, propagated, first, matrix, out, rows):
    parts = []
    for a in range(BLOCKS):
        for c in range(3):
            for p in range(2):
                value = first[c, p, a] - propagated[c, p, a]
                rows[c, p, a, pl.ds(0, 8, stride=2), :] = value
                rows[c, p, a, pl.ds(1, 8, stride=2), :] = value
    for a in range(BLOCKS):
        for c in range(3):
            parts.append(
                jnp.concatenate([fine_end[c, p, a] + rows[c, p // 2, a] for p in range(4)], axis=1)
            )
    natural = placed(jnp.concatenate(parts, axis=0), matrix[...])
    for a in range(BLOCKS):
        for c in range(3):
            base = (a * 3 + c) * ROWS
            out[c, :, a * 512 : (a + 1) * 512] = natural[base : base + ROWS]


def coarse_origin(offset):
    return lax.axis_index("tile") * (ROWS // 2) - offset, lax.axis_size("tile") * (ROWS // 2)


def coarse_planes():
    return [(c, p, a) for c in range(3) for p in range(2) for a in range(BLOCKS)]


def first_kernel(own, far, near, inverse, table, one, wide, height, height_new, flux, diff):
    odd = on_odd()
    for c, p, a in coarse_planes():
        to = height.at[p, a] if c == 0 else flux.at[c - 1, p, a]
        base = ((c * 2 + p) * BLOCKS + a) * COARSE_HALO
        distant = far[base : base + COARSE_HALO, :]
        close = near[base : base + COARSE_HALO, :]
        to[7:16, :] = jnp.where(odd, close, distant)
        to[16:24, :] = own[c, p, a]
        to[24:33, :] = jnp.where(odd, distant, close)
    wave_step(
        2, COARSE_NAMES, table, inverse, COARSE_RATIO, height, height_new, flux, diff,
        ((8, 24), (8, 24), (8, 24)), *coarse_origin(16),
    )
    for c, p, a in coarse_planes():
        result = height_new.at[p, a] if c == 0 else flux.at[c - 1, p, a]
        one[c, p, a] = result[16:24, :]
        wide[c, p, a] = result[8:32, :]


def rest_kernel(wide, one, inverse, table, two, mixed, last, height, height_new, flux, diff):
    for c, p, a in coarse_planes():
        to = height.at[p, a] if c == 0 else flux.at[c - 1, p, a]
        to[8:32, :] = wide[c, p, a]
    arguments = (2, COARSE_NAMES, table, inverse, COARSE_RATIO)
    wave_step(*arguments, height, height_new, flux, diff, ((8, 24), (12, 16), (12, 16)), *coarse_origin(16))
    for c, p, a in coarse_planes():
        result = height_new.at[p, a] if c == 0 else flux.at[c - 1, p, a]
        two[c, p, a] = result[16:24, :]
    wave_step(*arguments, height_new, height, flux, diff, ((12, 16), (12, 16), (16, 8)), *coarse_origin(16))
    start = lax.axis_index("cuts") == 0
    for c, p, a in coarse_planes():
        result = height.at[p, a] if c == 0 else flux.at[c - 1, p, a]
        mixed[c, p, a] = jnp.where(start, result[16:24, :], one[c, p, a])
        last[c, p, a] = one[c, p, a]


def final_kernel(base_end, second, third, fourth, matrix, out, rows, staged, sems):
    parts = []
    for a in range(BLOCKS):
        for c in range(3):
            pair = []
            for p in range(2):
                pair.append(second[c, p, a] + (third[c, p, a] + fourth[c, p, a]))
            parts.append(jnp.concatenate(pair, axis=1))
    spread = placed(jnp.concatenate(parts, axis=0), matrix[...])
    copies = []
    for a in range(BLOCKS):
        for c in range(3):
            base = (a * 3 + c) * 8
            for s in range(4):
                value = spread[base : base + 8, s * LANES : (s + 1) * LANES]
                rows[c, a * 4 + s, pl.ds(0, 8, stride=2), :] = value
                rows[c, a * 4 + s, pl.ds(1, 8, stride=2), :] = value
        for c in range(3):
            for s in range(4 * a, 4 * a + 4):
                cols = slice(s * LANES, (s + 1) * LANES)
                staged[c, :, cols] = base_end[c, :, cols] + rows[c, s]
        block = pl.ds(a * 512, 512)
        copies.append(pltpu.make_async_copy(staged.at[:, :, block], out.at[:, :, block], sems.at[a]))
        copies[-1].start()
    for copy in copies:
        copy.wait()


def f32(*shape):
    return jax.ShapeDtypeStruct(shape, jnp.float32)


def scratch(*shape):
    return pltpu.VMEM(shape, jnp.float32)


VMEM_SPEC = pl.BlockSpec(memory_space=pltpu.VMEM)
HBM_SPEC = pl.BlockSpec(memory_space=pltpu.HBM)


def in_hbm(array):
    return pltpu.with_memory_space_constraint(array, pltpu.HBM)


def call(kernel, ins, outs, scratches=(), name=None):
    return pl.pallas_call(
        kernel,
        in_specs=[HBM_SPEC if own else VMEM_SPEC for own in ins],
        out_shape=[shape for shape, _ in outs],
        out_specs=[HBM_SPEC if own else VMEM_SPEC for _, own in outs],
        scratch_shapes=scratches,
        name=name,
        compiler_params=pltpu.CompilerParams(vmem_limit_bytes=VMEM_LIMIT),
    )


def per_device(start_states):
    tiles = lax.axis_size("tile")
    far_pairs = [(i, j) for k in range(1, tiles - 1, 2) for i, j in ((k, k + 1), (k + 1, k))]
    near_pairs = [(i, i ^ 1) for i in range(tiles)]
    dma = pltpu.SemaphoreType.DMA

    halo = (f32(16 * HALO_ROWS, LANES), False)
    x, to_far, to_near = call(
        pack_kernel, [True], [(f32(3, ROWS, NX), False), halo, halo], [dma((3,))], name="pack"
    )(in_hbm(start_states[0]))
    far = lax.ppermute(to_far, "tile", far_pairs)
    near = lax.ppermute(to_near, "tile", near_pairs)
    fine_shape = (f32(3, 4, BLOCKS, ROWS, LANES), False)
    inverse_shape = (jax.ShapeDtypeStruct(FINE_INVERSE.shape, jnp.bfloat16), False)
    own, fine_inverse = call(
        own_kernel, [False, False, True], [fine_shape, inverse_shape], [dma(())], name="phases"
    )(x, PHASES, in_hbm(FINE_INVERSE))

    coarse = (f32(3, 2, BLOCKS, 8, LANES), False)
    coarse_halo = (f32(3 * 2 * BLOCKS * COARSE_HALO, LANES), False)
    fine_end, u_own, u_far, u_near, propagated = call(
        fine_kernel,
        [False] * 8,
        [fine_shape, coarse, coarse_halo, coarse_halo, coarse],
        [
            scratch(4, BLOCKS, 48, LANES),
            scratch(4, BLOCKS, 48, LANES),
            scratch(2, 4, BLOCKS, 48, LANES),
            scratch(2, 4, BLOCKS, 48, LANES),
            scratch(2, BLOCKS, 32, LANES),
            scratch(2, BLOCKS, 32, LANES),
            scratch(2, 2, BLOCKS, 32, LANES),
            scratch(2, 2, BLOCKS, 32, LANES),
        ],
        name="fine",
    )(own, far, near, PHASES, fine_inverse, COARSE_INVERSE, FINE_TABLE, COARSE_TABLE)

    u_far = lax.ppermute(u_far, "tile", far_pairs)
    u_near = lax.ppermute(u_near, "tile", near_pairs)

    state = [
        scratch(2, BLOCKS, 48, LANES),
        scratch(2, BLOCKS, 48, LANES),
        scratch(2, 2, BLOCKS, 48, LANES),
        scratch(2, 2, BLOCKS, 48, LANES),
    ]
    one, wide = call(
        first_kernel, [False] * 5, [coarse, (f32(3, 2, BLOCKS, 24, LANES), False)], state, name="first"
    )(u_own, u_far, u_near, COARSE_INVERSE, COARSE_TABLE)
    first = lax.ppermute(one, "cuts", [(0, 1)])
    two, mixed, last = call(rest_kernel, [False] * 4, [coarse] * 3, state, name="rest")(
        wide, one, COARSE_INVERSE, COARSE_TABLE
    )
    second = lax.ppermute(two, "cuts", [(0, 2), (1, 3)])
    third = lax.ppermute(mixed, "cuts", [(0, 3), (1, 2)])
    fourth = lax.ppermute(last, "cuts", [(2, 3)])
    (natural,) = call(
        natural_kernel,
        [False] * 4,
        [(f32(3, ROWS, NX), False)],
        [scratch(3, 2, BLOCKS, ROWS, LANES)],
        name="natural",
    )(fine_end, propagated, first, NATURAL)
    (out,) = call(
        final_kernel,
        [False] * 5,
        [(f32(3, ROWS, NX), True)],
        [scratch(3, 16, ROWS, LANES), scratch(3, ROWS, NX), dma((BLOCKS,))],
        name="final",
    )(natural, second, third, fourth, SPREAD)
    return out[None]


def solution(mesh):
    spec = P("cuts", None, "tile", None)
    return jax.shard_map(per_device, mesh=mesh, in_specs=(spec,), out_specs=spec, check_vma=False)
```

```python
import jax
import jax.numpy as jnp
import ml_dtypes
import numpy as np
from jax import lax
from jax.experimental import pallas as pl
from jax.experimental.pallas import tpu as pltpu
from jax.sharding import PartitionSpec as P

STEPS = 3
FINE_SPACING = 0.05
COARSE_SPACING = 0.1
FINE_STEP = 0.015
COARSE_STEP = 0.045

NX = 2048
ROWS = 16
UNKNOWNS = 512
BLOCKS = 4
LANES = 128
VMEM_LIMIT = 48 * 1024 * 1024


def halves(values):
    high = values.astype(np.float32).astype(ml_dtypes.bfloat16)
    low = (values - high.astype(np.float64)).astype(np.float32).astype(ml_dtypes.bfloat16)
    return high, low


def shifted(values):
    return np.concatenate([[0.0], values[:-1]])


def eliminated(lower, middle, upper):
    lower_e, lower_o = lower[0::2], lower[1::2]
    middle_e, middle_o = middle[0::2], middle[1::2]
    upper_e, upper_o = upper[0::2], upper[1::2]
    middle_n = np.append(middle_e[1:], 1.0)
    lower_n = np.append(lower_e[1:], 0.0)
    upper_n = np.append(upper_e[1:], 0.0)
    alpha = -lower_o / middle_e
    gamma = -upper_o / middle_n
    reduced = (alpha * lower_e, middle_o + alpha * upper_e + gamma * lower_n, gamma * upper_n)
    return alpha, gamma, reduced


def operator_tables(phases, columns, spacing, time_step):
    stride = NX // columns
    centers = (np.arange(columns) + 0.5) * stride
    depth = 0.9 + 0.3 * np.sin(6.0 * np.pi * centers / NX)
    beta = depth * depth / 3.0
    coupling = beta / (spacing * spacing)
    lower = -coupling.copy()
    lower[0] = 0.0
    upper = -coupling.copy()
    upper[-1] = 0.0
    middle = 1.0 + 2.0 * coupling
    slope = time_step * depth / (2.0 * spacing)
    weight = beta / (spacing * spacing + 4.0 * beta)
    rows = {}
    for p in range(phases):
        rows["slope", p] = slope[p::phases]
        rows["weight", p] = weight[p::phases]
        rows["centre", p] = 1.0 - 2.0 * weight[p::phases]
    alpha, gamma, first = eliminated(lower, middle, upper)
    if phases == 4:
        alpha2, gamma2, last = eliminated(*first)
        a1, a3, g1, g3 = alpha[0::2], alpha[1::2], gamma[0::2], gamma[1::2]
        rows["s0"] = alpha2 * a1
        rows["s1"] = alpha2
        rows["s2"] = a3 + alpha2 * g1
        rows["n1"] = shifted(gamma2)
        rows["n0"] = shifted(gamma2) * a1 + shifted(g3)
        rows["n2"] = shifted(gamma2) * g1
        l1, m1, u1 = (v[0::2] for v in first)
        rows["b1"] = 1.0 / m1
        rows["b0"] = a1 / m1
        rows["b2"] = g1 / m1
        rows["bp"] = -l1 / m1
        rows["b3"] = -u1 / m1
        rows["c0"] = 1.0 / middle[0::4]
        rows["cp"] = -lower[0::4] / middle[0::4]
        rows["c1"] = -upper[0::4] / middle[0::4]
        rows["d2"] = 1.0 / middle[2::4]
        rows["d1"] = -lower[2::4] / middle[2::4]
        rows["d3"] = -upper[2::4] / middle[2::4]
    else:
        last = first
        rows["s0"] = alpha
        rows["n0"] = shifted(gamma)
        rows["c0"] = 1.0 / middle[0::2]
        rows["cp"] = -lower[0::2] / middle[0::2]
        rows["c1"] = -upper[0::2] / middle[0::2]
    low, mid, up = last
    matrix = np.diag(mid) + np.diag(low[1:], -1) + np.diag(up[:-1], 1)
    inverse = np.linalg.inv(matrix)
    names = {name: i for i, name in enumerate(rows)}
    table = np.stack(list(rows.values())).reshape(-1, LANES).astype(np.float32)
    return names, table, np.stack(halves(inverse.T))


FINE_NAMES, FINE_TABLE, FINE_INVERSE = operator_tables(4, NX, FINE_SPACING, FINE_STEP)
COARSE_NAMES, COARSE_TABLE, COARSE_INVERSE = operator_tables(2, NX // 2, COARSE_SPACING, COARSE_STEP)


def phase_matrix():
    matrix = np.zeros((512, 512), np.float32)
    j = np.arange(512)
    matrix[j, (j % 4) * LANES + j // 4] = 1.0
    return matrix


PHASES = phase_matrix().astype(ml_dtypes.bfloat16)
NATURAL = phase_matrix().T.copy().astype(ml_dtypes.bfloat16)


def spread_matrix():
    matrix = np.zeros((256, 512), np.float32)
    c = np.arange(512)
    coarse = c // 2
    matrix[(coarse % 2) * LANES + coarse // 2, c] = 1.0
    return matrix


SPREAD = spread_matrix().astype(ml_dtypes.bfloat16)


def split(values):
    high = values.astype(jnp.bfloat16)
    low = (values - high.astype(jnp.float32)).astype(jnp.bfloat16)
    return high, low


def dot(a, b):
    return jnp.dot(a, b, preferred_element_type=jnp.float32)


def placed(values, matrix):
    count = values.shape[0]
    high, low = split(values)
    both = dot(jnp.concatenate([high, low], axis=0), matrix)
    return both[:count] + both[count:]


def lane_index(rows):
    return lax.broadcasted_iota(jnp.int32, (rows, LANES), 1)


def following(tiles):
    lane = lane_index(tiles[0].shape[0])
    rolled = [pltpu.roll(t, LANES - 1, 1) for t in tiles] + [jnp.zeros_like(tiles[0])]
    return [jnp.where(lane == LANES - 1, rolled[a + 1], rolled[a]) for a in range(BLOCKS)]


def preceding(tiles):
    lane = lane_index(tiles[0].shape[0])
    rolled = [jnp.zeros_like(tiles[0])] + [pltpu.roll(t, 1, 1) for t in tiles]
    return [jnp.where(lane == 0, rolled[a], rolled[a + 1]) for a in range(BLOCKS)]


def inside(first, count, total):
    row = lax.broadcasted_iota(jnp.int32, (count, LANES), 0) + first
    return jnp.where((row >= 0) & (row < total), 1.0, 0.0).astype(jnp.float32)


def step_stages(phases, names, table, inverse, ratio, height, height_new, flux, diff, windows, origin, total):
    (h0, hn), (d0, dn), ends = windows
    last = phases - 1

    def coef(name, a):
        i = names[name] * BLOCKS + a
        return table[i : i + 1, :]

    mask = inside(origin + h0, hn, total)
    rows = pl.ds(h0, hn)
    before = preceding([flux[0, last, a, rows, :] for a in range(BLOCKS)])
    after = following([flux[0, 0, a, rows, :] for a in range(BLOCKS)])
    for p in range(phases):
        for a in range(BLOCKS):
            right = after[a] if p == last else flux[0, p + 1, a, rows, :]
            left = before[a] if p == 0 else flux[0, p - 1, a, rows, :]
            down = flux[1, p, a, pl.ds(h0 + 1, hn), :]
            upper = flux[1, p, a, pl.ds(h0 - 1, hn), :]
            change = (right - left) + (down - upper)
            height_new[p, a, rows, :] = (height[p, a, rows, :] - ratio * change) * mask
    yield

    rows = pl.ds(d0, dn)
    mask = inside(origin + d0, dn, total)

    def reduce(i):
        if i == 0:
            before = preceding([height_new[last, a, rows, :] for a in range(BLOCKS)])
            after = following([height_new[0, a, rows, :] for a in range(BLOCKS)])
        own, passed = [], []
        for a in range(BLOCKS):
            force = []
            for p in range(phases):
                if i == 0:
                    right = after[a] if p == last else height_new[p + 1, a, rows, :]
                    left = before[a] if p == 0 else height_new[p - 1, a, rows, :]
                    value = flux[0, p, a, rows, :] - coef(("slope", p), a) * (right - left)
                else:
                    down = height_new[p, a, pl.ds(d0 + 1, dn), :]
                    upper = height_new[p, a, pl.ds(d0 - 1, dn), :]
                    value = (flux[1, p, a, rows, :] - coef(("slope", p), a) * (down - upper)) * mask
                if p < last:
                    diff[i, p, a, rows, :] = value
                force.append(value)
            kept = force[last] + coef("s0", a) * force[0]
            sent = coef("n0", a) * force[0]
            if phases == 4:
                kept = kept + coef("s1", a) * force[1] + coef("s2", a) * force[2]
                sent = sent + coef("n1", a) * force[1] + coef("n2", a) * force[2]
            own.append(kept)
            passed.append(sent)
        arrived = following(passed)
        return jnp.concatenate([own[a] + arrived[a] for a in range(BLOCKS)], axis=1)

    def expand(i, solved):
        ends = [solved[:, a * LANES : (a + 1) * LANES] for a in range(BLOCKS)]
        before = preceding(ends)
        for a in range(BLOCKS):
            end, prior = ends[a], before[a]
            f0 = diff[i, 0, a, rows, :]
            if phases == 4:
                f1 = diff[i, 1, a, rows, :]
                f2 = diff[i, 2, a, rows, :]
                x1 = (
                    coef("b1", a) * f1
                    + coef("b0", a) * f0
                    + coef("b2", a) * f2
                    + coef("bp", a) * prior
                    + coef("b3", a) * end
                )
                x0 = coef("c0", a) * f0 + coef("cp", a) * prior + coef("c1", a) * x1
                x2 = coef("d2", a) * f2 + coef("d1", a) * x1 + coef("d3", a) * end
                trial = [x0, x1, x2, end]
            else:
                trial = [coef("c0", a) * f0 + coef("cp", a) * prior + coef("c1", a) * end, end]
            for p in range(phases):
                diff[i, p, a, rows, :] = trial[p] - flux[i, p, a, rows, :]

    pair = [reduce(0), reduce(1)]
    yield
    solved = solve(jnp.concatenate(pair, axis=0), inverse)
    yield
    expand(0, solved[:dn])
    expand(1, solved[dn:])
    yield

    for i in range(2):
        o0, on = ends[i]
        mask = inside(origin + o0, on, total)
        rows = pl.ds(o0, on)
        for p in range(phases):
            for a in range(BLOCKS):
                middle = diff[i, p, a, rows, :]
                down = diff[i, p, a, pl.ds(o0 + 1, on), :]
                upper = diff[i, p, a, pl.ds(o0 - 1, on), :]
                sides = coef(("weight", p), a) * (down + upper)
                flux[i, p, a, rows, :] = (flux[i, p, a, rows, :] + coef(("centre", p), a) * middle + sides) * mask
    yield


def solve(right, inverse):
    count = right.shape[0]
    high, low = split(right)
    both = dot(jnp.concatenate([high, low], axis=0), inverse[0])
    return both[:count] + both[count:] + dot(high, inverse[1])


def wave_step(*arguments):
    for _ in step_stages(*arguments):
        pass


def wave_steps_in_turn(*steps):
    for _ in zip(*[step_stages(*arguments) for arguments in steps]):
        pass


FINE_RATIO = FINE_STEP / (2.0 * FINE_SPACING)
COARSE_RATIO = COARSE_STEP / (2.0 * COARSE_SPACING)


def on_odd():
    return lax.rem(lax.axis_index("tile"), 2) == 1


def planes(phases):
    return [(c, p, a) for c in range(3) for p in range(phases) for a in range(BLOCKS)]


SPILL = ((0, 8), (8, 8), (16, 9))
SPILL_ROWS = 25
NEAR_START = 24 * 14
SPARE = 8


def fetch(pairs, sems):
    copies = [pltpu.make_async_copy(source, target, sems.at[i]) for i, (source, target) in enumerate(pairs)]
    for copy in copies:
        copy.start()
    return copies


def at_tile(tile_rows, offset):
    return lax.axis_index("tile") * tile_rows - offset, lax.axis_size("tile") * tile_rows


def fine_kernel(
    x_hbm, matrix_hbm, fine_inverse_hbm, fine_table_hbm, coarse_inverse_hbm, coarse_table_hbm,
    own, spill_far, u_wide, u_far, u_near, u_cross, coarse_inverse,
    x, matrix, fine_inverse, fine_table, coarse_table, sems,
    height, height_new, flux, diff, c_height, c_height_new, c_flux, c_diff,
):
    copies = fetch(
        (
            (x_hbm, x),
            (matrix_hbm, matrix),
            (fine_table_hbm, fine_table),
            (coarse_table_hbm, coarse_table),
            (fine_inverse_hbm, fine_inverse),
            (coarse_inverse_hbm, coarse_inverse),
        ),
        sems,
    )
    for ref in (height, height_new, flux, diff):
        for edge in (pl.ds(0, 16), pl.ds(32, 16)):
            target = ref.at[..., edge, :]
            target[...] = jnp.zeros(target.shape, jnp.float32)
    for ref in (c_height, c_height_new, c_flux, c_diff):
        ref[...] = jnp.zeros(ref.shape, jnp.float32)
    copies[0].wait()
    copies[1].wait()

    parts = []
    for a in range(BLOCKS):
        for c in range(3):
            parts.append(x[c, :, a * 512 : (a + 1) * 512])
    phased = placed(jnp.concatenate(parts, axis=0), matrix[...])
    for c, p, a in planes(4):
        to = height.at[p, a] if c == 0 else flux.at[c - 1, p, a]
        base = (a * 3 + c) * ROWS
        to[16:32, :] = phased[base : base + ROWS, p * LANES : (p + 1) * LANES]

    def restricted(ref, p, a, first, count):
        total = None
        for q in (2 * p, 2 * p + 1):
            for r in (first, first + 1):
                part = ref(q, a)[pl.ds(r, count, stride=2), :]
                total = part if total is None else total + part
        return 0.25 * total

    for p in range(2):
        for a in range(BLOCKS):
            c_height[p, a, 12:20, :] = restricted(lambda q, b: height.at[q, b], p, a, 16, 8)
            for i in range(2):
                c_flux[i, p, a, 12:20, :] = restricted(lambda q, b: flux.at[i, q, b], p, a, 16, 8)
    for copy in copies[2:]:
        copy.wait()

    coarse_arguments = (
        2, COARSE_NAMES, coarse_table, coarse_inverse, COARSE_RATIO, c_height, c_height_new, c_flux, c_diff,
        ((8, 16), (8, 16), ((8, 16), (8, 16))), *at_tile(ROWS // 2, 12),
    )
    fine_arguments = (4, FINE_NAMES, fine_table, fine_inverse, FINE_RATIO)
    place = at_tile(ROWS, 16)
    wave_steps_in_turn(
        (*fine_arguments, height, height_new, flux, diff, ((12, 24), (12, 24), ((12, 24), (12, 24))), *place),
        coarse_arguments,
    )
    wave_step(*fine_arguments, height_new, height, flux, diff, ((12, 24), (8, 32), ((8, 32), (8, 32))), *place)
    wave_step(*fine_arguments, height, height_new, flux, diff, ((8, 32), (8, 32), ((8, 32), (4, 40))), *place)

    odd = on_odd()
    later = jnp.where(lax.axis_index("cuts") > 0, 1.0, 0.0).astype(jnp.float32)
    for n, (c, p, a) in enumerate(planes(2)):
        if c == 0:
            end = restricted(lambda q, b: height_new.at[q, b], p, a, 0, 24)
            step = c_height_new[p, a, 4:28, :]
        else:
            end = restricted(lambda q, b: flux.at[c - 1, q, b], p, a, 0, 24)
            step = c_flux[c - 1, p, a, 4:28, :]
        step = later * step
        u = end - step
        u_wide[c, p, a] = u
        c_diff[0, p, a, 4:28, :] = u
        to_next = c_diff[0, p, a, 11:25, :]
        to_previous = c_diff[0, p, a, 7:21, :]
        u_far[n * 14 : n * 14 + 14, :] = jnp.where(odd, to_next, to_previous)
        u_near[n * 14 : n * 14 + 14, :] = jnp.where(odd, to_previous, to_next)
        forward = c_diff[0, p, a, 19:25, :]
        backward = c_diff[0, p, a, 7:13, :]
        u_cross[n * 6 : n * 6 + 6, :] = jnp.where(odd, forward, backward)
    for c, p, a in planes(4):
        source = height_new.at[p, a] if c == 0 else flux.at[c - 1, p, a]
        step = c_height_new.at[p // 2, a] if c == 0 else c_flux.at[c - 1, p // 2, a]
        start, count = SPILL[c]
        base = (p * BLOCKS + a) * SPILL_ROWS + start
        for q in (0, 1):
            lines = pl.ds(8 + q, 16, stride=2)
            source[lines, :] = source[lines, :] - later * step[8:24, :]
        own[c, p, a] = source[16:32, :]
        to_next = source[32 : 32 + count, :]
        to_previous = source[16 - count : 16, :]
        spill_far[base : base + count, :] = jnp.where(odd, to_next, to_previous)
        base += NEAR_START
        u_near[base : base + count, :] = jnp.where(odd, to_previous, to_next)


def join_kernel(own, near, out):
    odd = on_odd()

    @pl.when(odd)
    def _():
        for n in range(24):
            base = n * 14
            out[base + 6 : base + 14, :] = own[base + 6 : base + 14, :]
            out[base : base + 6, :] = own[base : base + 6, :] + near[base + 8 : base + 14, :]

    @pl.when(jnp.logical_not(odd))
    def _():
        for n in range(24):
            base = n * 14
            out[base : base + 8, :] = own[base : base + 8, :]
            out[base + 8 : base + 14, :] = own[base + 8 : base + 14, :] + near[base : base + 6, :]


def later_kernel(rows, arrived, out):
    out[...] = rows[...]


def first_kernel(
    own, far, near, cross, inverse, table, one, wide, height, height_new, flux, diff
):
    odd = on_odd()
    for n, (c, p, a) in enumerate(planes(2)):
        to = height.at[p, a] if c == 0 else flux.at[c - 1, p, a]
        distant = far[n * 14 : n * 14 + 14, :]
        close = near[n * 14 : n * 14 + 14, :]
        to[0:8, :] = jnp.zeros((8, LANES), jnp.float32)
        to[8:32, :] = own[c, p, a]
        to[32:40, :] = jnp.zeros((8, LANES), jnp.float32)
        to[7:21, :] = to[7:21, :] + jnp.where(odd, close, distant)
        to[19:33, :] = to[19:33, :] + jnp.where(odd, distant, close)
        beyond = cross[n * 6 : n * 6 + 6, :]
        to[7:13, :] = to[7:13, :] + jnp.where(odd, beyond, 0.0)
        to[27:33, :] = to[27:33, :] + jnp.where(odd, 0.0, beyond)
    window = (8, 24)
    wave_step(
        2, COARSE_NAMES, table, inverse, COARSE_RATIO, height, height_new, flux, diff,
        (window, window, (window, window)), *at_tile(ROWS // 2, 16),
    )
    for c, p, a in planes(2):
        result = height_new.at[p, a] if c == 0 else flux.at[c - 1, p, a]
        one[c, p, a] = result[16:24, :]
        wide[c, p, a] = result[8:32, :]


def rest_kernel(wide, one, inverse, table, early, two, mixed, last, height, height_new, flux, diff):
    for c, p, a in planes(2):
        to = height.at[p, a] if c == 0 else flux.at[c - 1, p, a]
        to[8:32, :] = wide[c, p, a]
    arguments = (2, COARSE_NAMES, table, inverse, COARSE_RATIO)
    wave_step(*arguments, height, height_new, flux, diff, ((8, 24), (12, 16), ((12, 16), (12, 16))), *at_tile(ROWS // 2, 16))
    for c, p, a in planes(2):
        result = height_new.at[p, a] if c == 0 else flux.at[c - 1, p, a]
        two[c, p, a] = result[16:24, :]
    wave_step(*arguments, height_new, height, flux, diff, ((12, 16), (12, 16), ((16, 8), (16, 8))), *at_tile(ROWS // 2, 16))
    start = lax.axis_index("cuts") == 0
    for c, p, a in planes(2):
        result = height.at[p, a] if c == 0 else flux.at[c - 1, p, a]
        mixed[c, p, a] = jnp.where(start, result[16:24, :], one[c, p, a])
        last[c, p, a] = one[c, p, a]
        early[c, p, a] = one[c, p, a]


def natural_kernel(own, far, near, first, matrix, out, rows, total):
    odd = on_odd()
    for c, p, a in planes(2):
        rows[c, p, a, pl.ds(0, 8, stride=2), :] = first[c, p, a]
        rows[c, p, a, pl.ds(1, 8, stride=2), :] = first[c, p, a]
    for c, p, a in planes(4):
        start, count = SPILL[c]
        base = (p * BLOCKS + a) * SPILL_ROWS + start
        distant = far[base : base + count, :]
        close = near[NEAR_START + base : NEAR_START + base + count, :]
        to = total.at[c, p, a]
        to[0:ROWS, :] = own[c, p, a] + rows[c, p // 2, a]
        to[0:count, :] = to[0:count, :] + jnp.where(odd, close, distant)
        to[ROWS - count : ROWS, :] = to[ROWS - count : ROWS, :] + jnp.where(odd, distant, close)
    parts = []
    for a in range(BLOCKS):
        for c in range(3):
            parts.append(jnp.concatenate([total[c, p, a, 0:ROWS, :] for p in range(4)], axis=1))
    natural = placed(jnp.concatenate(parts, axis=0), matrix[...])
    for a in range(BLOCKS):
        for c in range(3):
            base = (a * 3 + c) * ROWS
            out[c, :, a * 512 : (a + 1) * 512] = natural[base : base + ROWS]


def final_kernel(base_end, second, third, fourth, matrix, out, rows, staged, sems):
    parts = []
    for a in range(BLOCKS):
        for c in range(3):
            pair = []
            for p in range(2):
                pair.append(second[c, p, a] + (third[c, p, a] + fourth[c, p, a]))
            parts.append(jnp.concatenate(pair, axis=1))
    spread = placed(jnp.concatenate(parts, axis=0), matrix[...])
    copies = []
    for a in range(BLOCKS):
        for c in range(3):
            base = (a * 3 + c) * 8
            for s in range(4):
                value = spread[base : base + 8, s * LANES : (s + 1) * LANES]
                rows[c, a * 4 + s, pl.ds(0, 8, stride=2), :] = value
                rows[c, a * 4 + s, pl.ds(1, 8, stride=2), :] = value
        for c in range(3):
            for s in range(4 * a, 4 * a + 4):
                cols = slice(s * LANES, (s + 1) * LANES)
                staged[c, :, cols] = base_end[c, :, cols] + rows[c, s]
        block = pl.ds(a * 512, 512)
        copies.append(pltpu.make_async_copy(staged.at[:, :, block], out.at[:, :, block], sems.at[a]))
        copies[-1].start()
    for copy in copies:
        copy.wait()


def f32(*shape):
    return jax.ShapeDtypeStruct(shape, jnp.float32)


def scratch(*shape):
    return pltpu.VMEM(shape, jnp.float32)


VMEM_SPEC = pl.BlockSpec(memory_space=pltpu.VMEM)
HBM_SPEC = pl.BlockSpec(memory_space=pltpu.HBM)


def in_hbm(array):
    return pltpu.with_memory_space_constraint(array, pltpu.HBM)


def call(kernel, ins, outs, scratches=(), name=None):
    return pl.pallas_call(
        kernel,
        in_specs=[HBM_SPEC if own else VMEM_SPEC for own in ins],
        out_shape=[shape for shape, _ in outs],
        out_specs=[HBM_SPEC if own else VMEM_SPEC for _, own in outs],
        scratch_shapes=scratches,
        name=name,
        compiler_params=pltpu.CompilerParams(vmem_limit_bytes=VMEM_LIMIT),
    )


def per_device(start_states):
    tiles = lax.axis_size("tile")
    far_pairs = [(i, j) for k in range(1, tiles - 1, 2) for i, j in ((k, k + 1), (k + 1, k))]
    near_pairs = [(i, i ^ 1) for i in range(tiles)]
    cross_pairs = [(i, i + 2) if i % 2 else (i + 2, i) for i in range(tiles - 2)]
    dma = pltpu.SemaphoreType.DMA

    def bf16(array):
        return jax.ShapeDtypeStruct(array.shape, jnp.bfloat16)

    def here(array):
        return pltpu.VMEM(array.shape, array.dtype)

    coarse = (f32(3, 2, BLOCKS, 8, LANES), False)
    spilt = (f32(16 * SPILL_ROWS + SPARE, LANES), False)
    far_rows = (f32(NEAR_START + SPARE, LANES), False)
    next_rows = (f32(24 * 6 + SPARE, LANES), False)
    fetched = (start_states[0], PHASES, FINE_INVERSE, FINE_TABLE, COARSE_INVERSE, COARSE_TABLE)
    own, spill_far, u_wide, u_far, near, cross, coarse_inverse = call(
        fine_kernel,
        [True] * 6,
        [
            (f32(3, 4, BLOCKS, ROWS, LANES), False),
            spilt,
            (f32(3, 2, BLOCKS, 24, LANES), False),
            far_rows,
            (f32(NEAR_START + 16 * SPILL_ROWS + SPARE, LANES), False),
            next_rows,
            (bf16(COARSE_INVERSE), False),
        ],
        [
            scratch(3, ROWS, NX),
            here(PHASES),
            here(FINE_INVERSE),
            here(FINE_TABLE),
            here(COARSE_TABLE),
            dma((6,)),
            scratch(4, BLOCKS, 48, LANES),
            scratch(4, BLOCKS, 48, LANES),
            scratch(2, 4, BLOCKS, 48, LANES),
            scratch(2, 4, BLOCKS, 48, LANES),
            scratch(2, BLOCKS, 32, LANES),
            scratch(2, BLOCKS, 32, LANES),
            scratch(2, 2, BLOCKS, 32, LANES),
            scratch(2, 2, BLOCKS, 32, LANES),
        ],
        name="fine",
    )(*[in_hbm(array) for array in fetched])
    near = lax.ppermute(near, "tile", near_pairs)
    cross = lax.ppermute(cross, "tile", cross_pairs)
    (u_far,) = call(join_kernel, [False] * 2, [far_rows], name="join")(u_far, near)
    u_far = lax.ppermute(u_far, "tile", far_pairs)
    (spill_far,) = call(later_kernel, [False] * 2, [spilt], name="later")(spill_far, cross)
    spill_far = lax.ppermute(spill_far, "tile", far_pairs)

    state = [
        scratch(2, BLOCKS, 48, LANES),
        scratch(2, BLOCKS, 48, LANES),
        scratch(2, 2, BLOCKS, 48, LANES),
        scratch(2, 2, BLOCKS, 48, LANES),
    ]
    one, wide = call(
        first_kernel, [False] * 6, [coarse, (f32(3, 2, BLOCKS, 24, LANES), False)], state, name="first"
    )(u_wide, u_far, near, cross, coarse_inverse, COARSE_TABLE)
    early, two, mixed, last = call(rest_kernel, [False] * 4, [coarse] * 4, state, name="rest")(
        wide, one, coarse_inverse, COARSE_TABLE
    )
    first = lax.ppermute(early, "cuts", [(0, 1)])
    second = lax.ppermute(two, "cuts", [(0, 2), (1, 3)])
    third = lax.ppermute(mixed, "cuts", [(0, 3), (1, 2)])
    fourth = lax.ppermute(last, "cuts", [(2, 3)])
    (natural,) = call(
        natural_kernel,
        [False] * 5,
        [(f32(3, ROWS, NX), False)],
        [scratch(3, 2, BLOCKS, ROWS, LANES), scratch(3, 4, BLOCKS, ROWS + SPARE, LANES)],
        name="natural",
    )(own, spill_far, near, first, NATURAL)
    (out,) = call(
        final_kernel,
        [False] * 5,
        [(f32(3, ROWS, NX), True)],
        [scratch(3, 16, ROWS, LANES), scratch(3, ROWS, NX), dma((BLOCKS,))],
        name="final",
    )(natural, second, third, fourth, SPREAD)
    return out[None]


def solution(mesh):
    spec = P("cuts", None, "tile", None)
    return jax.shard_map(per_device, mesh=mesh, in_specs=(spec,), out_specs=spec, check_vma=False)
```

```python
import jax
import jax.numpy as jnp
import ml_dtypes
import numpy as np
from jax import lax
from jax.experimental import pallas as pl
from jax.experimental.pallas import tpu as pltpu
from jax.sharding import PartitionSpec as P

STEPS = 3
FINE_SPACING = 0.05
COARSE_SPACING = 0.1
FINE_STEP = 0.015
COARSE_STEP = 0.045

NX = 2048
ROWS = 16
UNKNOWNS = 512
BLOCKS = 4
LANES = 128
COST = 10**10
VMEM_LIMIT = 48 * 1024 * 1024


def halves(values):
    high = values.astype(np.float32).astype(ml_dtypes.bfloat16)
    low = (values - high.astype(np.float64)).astype(np.float32).astype(ml_dtypes.bfloat16)
    return high, low


def shifted(values):
    return np.concatenate([[0.0], values[:-1]])


def eliminated(lower, middle, upper):
    lower_e, lower_o = lower[0::2], lower[1::2]
    middle_e, middle_o = middle[0::2], middle[1::2]
    upper_e, upper_o = upper[0::2], upper[1::2]
    middle_n = np.append(middle_e[1:], 1.0)
    lower_n = np.append(lower_e[1:], 0.0)
    upper_n = np.append(upper_e[1:], 0.0)
    alpha = -lower_o / middle_e
    gamma = -upper_o / middle_n
    reduced = (alpha * lower_e, middle_o + alpha * upper_e + gamma * lower_n, gamma * upper_n)
    return alpha, gamma, reduced


def operator_tables(phases, columns, spacing, time_step):
    stride = NX // columns
    centers = (np.arange(columns) + 0.5) * stride
    depth = 0.9 + 0.3 * np.sin(6.0 * np.pi * centers / NX)
    beta = depth * depth / 3.0
    coupling = beta / (spacing * spacing)
    lower = -coupling.copy()
    lower[0] = 0.0
    upper = -coupling.copy()
    upper[-1] = 0.0
    middle = 1.0 + 2.0 * coupling
    slope = time_step * depth / (2.0 * spacing)
    weight = beta / (spacing * spacing + 4.0 * beta)
    rows = {}
    for p in range(phases):
        rows["slope", p] = slope[p::phases]
        rows["weight", p] = weight[p::phases]
        rows["centre", p] = 1.0 - 2.0 * weight[p::phases]
    alpha, gamma, first = eliminated(lower, middle, upper)
    if phases == 4:
        alpha2, gamma2, last = eliminated(*first)
        a1, a3, g1, g3 = alpha[0::2], alpha[1::2], gamma[0::2], gamma[1::2]
        rows["s0"] = alpha2 * a1
        rows["s1"] = alpha2
        rows["s2"] = a3 + alpha2 * g1
        rows["n1"] = shifted(gamma2)
        rows["n0"] = shifted(gamma2) * a1 + shifted(g3)
        rows["n2"] = shifted(gamma2) * g1
        l1, m1, u1 = (v[0::2] for v in first)
        rows["b1"] = 1.0 / m1
        rows["b0"] = a1 / m1
        rows["b2"] = g1 / m1
        rows["bp"] = -l1 / m1
        rows["b3"] = -u1 / m1
        rows["c0"] = 1.0 / middle[0::4]
        rows["cp"] = -lower[0::4] / middle[0::4]
        rows["c1"] = -upper[0::4] / middle[0::4]
        rows["d2"] = 1.0 / middle[2::4]
        rows["d1"] = -lower[2::4] / middle[2::4]
        rows["d3"] = -upper[2::4] / middle[2::4]
    else:
        last = first
        rows["s0"] = alpha
        rows["n0"] = shifted(gamma)
        rows["c0"] = 1.0 / middle[0::2]
        rows["cp"] = -lower[0::2] / middle[0::2]
        rows["c1"] = -upper[0::2] / middle[0::2]
    low, mid, up = last
    matrix = np.diag(mid) + np.diag(low[1:], -1) + np.diag(up[:-1], 1)
    inverse = np.linalg.inv(matrix)
    names = {name: i for i, name in enumerate(rows)}
    table = np.stack(list(rows.values())).reshape(-1, LANES).astype(np.float32)
    return names, table, np.stack(halves(inverse.T))


FINE_NAMES, FINE_TABLE, FINE_INVERSE = operator_tables(4, NX, FINE_SPACING, FINE_STEP)
COARSE_NAMES, COARSE_TABLE, COARSE_INVERSE = operator_tables(2, NX // 2, COARSE_SPACING, COARSE_STEP)


def phase_matrix():
    matrix = np.zeros((512, 512), np.float32)
    j = np.arange(512)
    matrix[j, (j % 4) * LANES + j // 4] = 1.0
    return matrix


NATURAL = phase_matrix().T.copy().astype(ml_dtypes.bfloat16)


def spread_matrix():
    matrix = np.zeros((256, 512), np.float32)
    c = np.arange(512)
    coarse = c // 2
    matrix[(coarse % 2) * LANES + coarse // 2, c] = 1.0
    return matrix


SPREAD = spread_matrix().astype(ml_dtypes.bfloat16)


def split(values):
    high = values.astype(jnp.bfloat16)
    low = (values - high.astype(jnp.float32)).astype(jnp.bfloat16)
    return high, low


def dot(a, b):
    return jnp.dot(a, b, preferred_element_type=jnp.float32)


def placed(values, matrix):
    count = values.shape[0]
    high, low = split(values)
    both = dot(jnp.concatenate([high, low], axis=0), matrix)
    return both[:count] + both[count:]


def lane_index(rows):
    return lax.broadcasted_iota(jnp.int32, (rows, LANES), 1)


def following(tiles):
    lane = lane_index(tiles[0].shape[0])
    rolled = [pltpu.roll(t, LANES - 1, 1) for t in tiles] + [jnp.zeros_like(tiles[0])]
    return [jnp.where(lane == LANES - 1, rolled[a + 1], rolled[a]) for a in range(BLOCKS)]


def preceding(tiles):
    lane = lane_index(tiles[0].shape[0])
    rolled = [jnp.zeros_like(tiles[0])] + [pltpu.roll(t, 1, 1) for t in tiles]
    return [jnp.where(lane == 0, rolled[a], rolled[a + 1]) for a in range(BLOCKS)]


def inside(first, count, total):
    row = lax.broadcasted_iota(jnp.int32, (count, LANES), 0) + first
    return jnp.where((row >= 0) & (row < total), 1.0, 0.0).astype(jnp.float32)


def step_stages(phases, names, table, inverse, ratio, height, height_new, flux, diff, windows, origin, total):
    (h0, hn), (d0, dn), ends = windows
    last = phases - 1

    def coef(name, a):
        i = names[name] * BLOCKS + a
        return table[i : i + 1, :]

    mask = inside(origin + h0, hn, total)
    rows = pl.ds(h0, hn)
    before = preceding([flux[0, last, a, rows, :] for a in range(BLOCKS)])
    after = following([flux[0, 0, a, rows, :] for a in range(BLOCKS)])
    for p in range(phases):
        for a in range(BLOCKS):
            right = after[a] if p == last else flux[0, p + 1, a, rows, :]
            left = before[a] if p == 0 else flux[0, p - 1, a, rows, :]
            down = flux[1, p, a, pl.ds(h0 + 1, hn), :]
            upper = flux[1, p, a, pl.ds(h0 - 1, hn), :]
            change = (right - left) + (down - upper)
            height_new[p, a, rows, :] = (height[p, a, rows, :] - ratio * change) * mask
    yield

    rows = pl.ds(d0, dn)
    mask = inside(origin + d0, dn, total)

    def reduce(i):
        if i == 0:
            before = preceding([height_new[last, a, rows, :] for a in range(BLOCKS)])
            after = following([height_new[0, a, rows, :] for a in range(BLOCKS)])
        own, passed = [], []
        for a in range(BLOCKS):
            force = []
            for p in range(phases):
                if i == 0:
                    right = after[a] if p == last else height_new[p + 1, a, rows, :]
                    left = before[a] if p == 0 else height_new[p - 1, a, rows, :]
                    value = flux[0, p, a, rows, :] - coef(("slope", p), a) * (right - left)
                else:
                    down = height_new[p, a, pl.ds(d0 + 1, dn), :]
                    upper = height_new[p, a, pl.ds(d0 - 1, dn), :]
                    value = (flux[1, p, a, rows, :] - coef(("slope", p), a) * (down - upper)) * mask
                if p < last:
                    diff[i, p, a, rows, :] = value
                force.append(value)
            kept = force[last] + coef("s0", a) * force[0]
            sent = coef("n0", a) * force[0]
            if phases == 4:
                kept = kept + coef("s1", a) * force[1] + coef("s2", a) * force[2]
                sent = sent + coef("n1", a) * force[1] + coef("n2", a) * force[2]
            own.append(kept)
            passed.append(sent)
        arrived = following(passed)
        return jnp.concatenate([own[a] + arrived[a] for a in range(BLOCKS)], axis=1)

    def expand(i, solved):
        ends = [solved[:, a * LANES : (a + 1) * LANES] for a in range(BLOCKS)]
        before = preceding(ends)
        for a in range(BLOCKS):
            end, prior = ends[a], before[a]
            f0 = diff[i, 0, a, rows, :]
            if phases == 4:
                f1 = diff[i, 1, a, rows, :]
                f2 = diff[i, 2, a, rows, :]
                x1 = (
                    coef("b1", a) * f1
                    + coef("b0", a) * f0
                    + coef("b2", a) * f2
                    + coef("bp", a) * prior
                    + coef("b3", a) * end
                )
                x0 = coef("c0", a) * f0 + coef("cp", a) * prior + coef("c1", a) * x1
                x2 = coef("d2", a) * f2 + coef("d1", a) * x1 + coef("d3", a) * end
                trial = [x0, x1, x2, end]
            else:
                trial = [coef("c0", a) * f0 + coef("cp", a) * prior + coef("c1", a) * end, end]
            for p in range(phases):
                diff[i, p, a, rows, :] = trial[p] - flux[i, p, a, rows, :]

    pair = [reduce(0), reduce(1)]
    yield
    solved = solve(jnp.concatenate(pair, axis=0), inverse)
    yield
    expand(0, solved[:dn])
    expand(1, solved[dn:])
    yield

    for i in range(2):
        o0, on = ends[i]
        mask = inside(origin + o0, on, total)
        rows = pl.ds(o0, on)
        for p in range(phases):
            for a in range(BLOCKS):
                middle = diff[i, p, a, rows, :]
                down = diff[i, p, a, pl.ds(o0 + 1, on), :]
                upper = diff[i, p, a, pl.ds(o0 - 1, on), :]
                sides = coef(("weight", p), a) * (down + upper)
                flux[i, p, a, rows, :] = (flux[i, p, a, rows, :] + coef(("centre", p), a) * middle + sides) * mask
    yield


def solve(right, inverse):
    count = right.shape[0]
    high, low = split(right)
    both = dot(jnp.concatenate([high, low], axis=0), inverse[0])
    return both[:count] + both[count:] + dot(high, inverse[1])


def wave_step(*arguments):
    for _ in step_stages(*arguments):
        pass


FINE_RATIO = FINE_STEP / (2.0 * FINE_SPACING)
COARSE_RATIO = COARSE_STEP / (2.0 * COARSE_SPACING)


def on_odd():
    return lax.rem(lax.axis_index("tile"), 2) == 1


def planes(phases):
    return [(c, p, a) for c in range(3) for p in range(phases) for a in range(BLOCKS)]


SPILL = ((0, 8), (8, 8), (16, 9))
SPILL_ROWS = 25
FAR_ROWS = 24 * 14
NEXT_ROWS = 24 * 6
SPARE = 8


def fetch(pairs, sems):
    copies = [pltpu.make_async_copy(source, target, sems.at[i]) for i, (source, target) in enumerate(pairs)]
    for copy in copies:
        copy.start()
    return copies


def at_tile(tile_rows, offset):
    return lax.axis_index("tile") * tile_rows - offset, lax.axis_size("tile") * tile_rows


def fine_kernel(
    x_hbm, fine_inverse_hbm, fine_table_hbm, coarse_inverse_hbm, coarse_table_hbm,
    wide_end, propagated, u_wide, u_far, u_near, coarse_inverse,
    x, matrix, fine_inverse, fine_table, coarse_table, sems,
    height, height_new, flux, diff, c_height, c_height_new, c_flux, c_diff,
):
    copies = fetch(
        (
            (x_hbm, x),
            (fine_table_hbm, fine_table),
            (coarse_table_hbm, coarse_table),
            (fine_inverse_hbm, fine_inverse),
            (coarse_inverse_hbm, coarse_inverse),
        ),
        sems,
    )
    for ref in (height, height_new, flux, diff):
        for edge in (pl.ds(0, 16), pl.ds(32, 16)):
            target = ref.at[..., edge, :]
            target[...] = jnp.zeros(target.shape, jnp.float32)
    for ref in (c_height, c_height_new, c_flux, c_diff):
        ref[...] = jnp.zeros(ref.shape, jnp.float32)
    row = lax.broadcasted_iota(jnp.int32, (512, 512), 0)
    column = lax.broadcasted_iota(jnp.int32, (512, 512), 1)
    chosen = column == (row & 3) * LANES + (row >> 2)
    matrix[...] = jnp.where(chosen, 1.0, 0.0).astype(jnp.bfloat16)
    copies[0].wait()

    parts = []
    for a in range(BLOCKS):
        for c in range(3):
            parts.append(x[c, :, a * 512 : (a + 1) * 512])
    phased = placed(jnp.concatenate(parts, axis=0), matrix[...])
    for c, p, a in planes(4):
        to = height.at[p, a] if c == 0 else flux.at[c - 1, p, a]
        base = (a * 3 + c) * ROWS
        to[16:32, :] = phased[base : base + ROWS, p * LANES : (p + 1) * LANES]

    def restricted(ref, p, a, first, count):
        total = None
        for q in (2 * p, 2 * p + 1):
            for r in (first, first + 1):
                part = ref(q, a)[pl.ds(r, count, stride=2), :]
                total = part if total is None else total + part
        return 0.25 * total

    for p in range(2):
        for a in range(BLOCKS):
            c_height[p, a, 12:20, :] = restricted(lambda q, b: height.at[q, b], p, a, 16, 8)
            for i in range(2):
                c_flux[i, p, a, 12:20, :] = restricted(lambda q, b: flux.at[i, q, b], p, a, 16, 8)
    for copy in copies[1:3]:
        copy.wait()

    coarse_arguments = (
        2, COARSE_NAMES, coarse_table, coarse_inverse, COARSE_RATIO, c_height, c_height_new, c_flux, c_diff,
        ((8, 16), (8, 16), ((8, 16), (8, 16))), *at_tile(ROWS // 2, 12),
    )
    fine_arguments = (4, FINE_NAMES, fine_table, fine_inverse, FINE_RATIO)
    place = at_tile(ROWS, 16)
    windows = ((12, 24), (12, 24), ((12, 24), (12, 24)))
    stages = (
        step_stages(*fine_arguments, height, height_new, flux, diff, windows, *place),
        step_stages(*coarse_arguments),
    )
    for _ in range(2):
        for stage in stages:
            next(stage)
    for copy in copies[3:]:
        copy.wait()
    for _ in zip(*stages):
        pass
    wave_step(*fine_arguments, height_new, height, flux, diff, ((12, 24), (8, 32), ((8, 32), (8, 32))), *place)
    wave_step(*fine_arguments, height, height_new, flux, diff, ((8, 32), (8, 32), ((8, 32), (4, 40))), *place)

    odd = on_odd()
    later = jnp.where(lax.axis_index("cuts") > 0, 1.0, 0.0).astype(jnp.float32)
    for n, (c, p, a) in enumerate(planes(2)):
        if c == 0:
            end = restricted(lambda q, b: height_new.at[q, b], p, a, 0, 24)
            step = c_height_new[p, a, 4:28, :]
        else:
            end = restricted(lambda q, b: flux.at[c - 1, q, b], p, a, 0, 24)
            step = c_flux[c - 1, p, a, 4:28, :]
        step = later * step
        propagated[c, p, a] = step[4:20]
        u = end - step
        u_wide[c, p, a] = u
        c_diff[0, p, a, 4:28, :] = u
        to_next = c_diff[0, p, a, 11:25, :]
        to_previous = c_diff[0, p, a, 7:21, :]
        u_far[n * 14 : n * 14 + 14, :] = jnp.where(odd, to_next, to_previous)
        u_near[n * 14 : n * 14 + 14, :] = jnp.where(odd, to_previous, to_next)
    for c, p, a in planes(4):
        source = height_new.at[p, a] if c == 0 else flux.at[c - 1, p, a]
        wide_end[c, p, a] = source[4:44, :]


def spill_kernel(wide_end, propagated, arrived, own, to_far, to_near, rows):
    del arrived
    odd = on_odd()
    for c, p, a in planes(2):
        value = propagated[c, p, a]
        rows[c, p, a, pl.ds(0, 16, stride=2), :] = value
        rows[c, p, a, pl.ds(1, 16, stride=2), :] = value
    for c, p, a in planes(4):
        start, count = SPILL[c]
        base = (p * BLOCKS + a) * SPILL_ROWS + start
        wide_end[c, p, a, 4:36, :] = wide_end[c, p, a, 4:36, :] - rows[c, p // 2, a]
        own[c, p, a] = wide_end[c, p, a, 12:28, :]
        to_next = wide_end[c, p, a, 28 : 28 + count, :]
        to_previous = wide_end[c, p, a, 12 - count : 12, :]
        to_far[base : base + count, :] = jnp.where(odd, to_next, to_previous)
        to_near[base : base + count, :] = jnp.where(odd, to_previous, to_next)


def join_kernel(own, near, out):
    odd = on_odd()

    @pl.when(odd)
    def _():
        for n in range(24):
            base = n * 14
            out[base + 6 : base + 14, :] = own[base + 6 : base + 14, :]
            out[base : base + 6, :] = own[base : base + 6, :] + near[base + 8 : base + 14, :]

    @pl.when(jnp.logical_not(odd))
    def _():
        for n in range(24):
            base = n * 14
            out[base : base + 8, :] = own[base : base + 8, :]
            out[base + 8 : base + 14, :] = own[base + 8 : base + 14, :] + near[base : base + 6, :]


def forward_kernel(far, rows, out):
    odd = on_odd()
    for n in range(24):
        low = far[n * 14 : n * 14 + 6, :]
        high = far[n * 14 + 8 : n * 14 + 14, :]
        out[n * 6 : n * 6 + 6, :] = jnp.where(odd, low, high)
    out[NEXT_ROWS : NEXT_ROWS + 16 * SPILL_ROWS, :] = rows[0 : 16 * SPILL_ROWS, :]


def assemble_kernel(own, far, near, out):
    odd = on_odd()
    for n, (c, p, a) in enumerate(planes(2)):
        to = out.at[c, p, a]
        distant = far[n * 14 : n * 14 + 14, :]
        close = near[n * 14 : n * 14 + 14, :]
        to[0:8, :] = jnp.zeros((8, LANES), jnp.float32)
        to[8:32, :] = own[c, p, a]
        to[32:40, :] = jnp.zeros((8, LANES), jnp.float32)
        to[7:21, :] = to[7:21, :] + jnp.where(odd, close, distant)
        to[19:33, :] = to[19:33, :] + jnp.where(odd, distant, close)


def first_kernel(assembled, cross, inverse, table, one, wide, height, height_new, flux, diff):
    odd = on_odd()
    for n, (c, p, a) in enumerate(planes(2)):
        to = height.at[p, a] if c == 0 else flux.at[c - 1, p, a]
        beyond = cross[n * 6 : n * 6 + 6, :]
        to[0:40, :] = assembled[c, p, a, 0:40, :]
        to[7:13, :] = to[7:13, :] + jnp.where(odd, beyond, 0.0)
        to[27:33, :] = to[27:33, :] + jnp.where(odd, 0.0, beyond)
    window = (8, 24)
    wave_step(
        2, COARSE_NAMES, table, inverse, COARSE_RATIO, height, height_new, flux, diff,
        (window, window, (window, window)), *at_tile(ROWS // 2, 16),
    )
    for c, p, a in planes(2):
        result = height_new.at[p, a] if c == 0 else flux.at[c - 1, p, a]
        one[c, p, a] = result[16:24, :]
        wide[c, p, a] = result[8:32, :]


def rest_kernel(wide, one, inverse, table, early, two, mixed, last, height, height_new, flux, diff):
    for c, p, a in planes(2):
        to = height.at[p, a] if c == 0 else flux.at[c - 1, p, a]
        to[8:32, :] = wide[c, p, a]
    arguments = (2, COARSE_NAMES, table, inverse, COARSE_RATIO)
    wave_step(*arguments, height, height_new, flux, diff, ((8, 24), (12, 16), ((12, 16), (12, 16))), *at_tile(ROWS // 2, 16))
    for c, p, a in planes(2):
        result = height_new.at[p, a] if c == 0 else flux.at[c - 1, p, a]
        two[c, p, a] = result[16:24, :]
    wave_step(*arguments, height_new, height, flux, diff, ((12, 16), (12, 16), ((16, 8), (16, 8))), *at_tile(ROWS // 2, 16))
    start = lax.axis_index("cuts") == 0
    for c, p, a in planes(2):
        result = height.at[p, a] if c == 0 else flux.at[c - 1, p, a]
        mixed[c, p, a] = jnp.where(start, result[16:24, :], one[c, p, a])
        last[c, p, a] = one[c, p, a]
        early[c, p, a] = one[c, p, a]


def natural_kernel(own, far, near, first, matrix, out, rows, total):
    odd = on_odd()
    for c, p, a in planes(2):
        rows[c, p, a, pl.ds(0, 8, stride=2), :] = first[c, p, a]
        rows[c, p, a, pl.ds(1, 8, stride=2), :] = first[c, p, a]
    for c, p, a in planes(4):
        start, count = SPILL[c]
        base = (p * BLOCKS + a) * SPILL_ROWS + start
        distant = far[base : base + count, :]
        close = near[NEXT_ROWS + base : NEXT_ROWS + base + count, :]
        to = total.at[c, p, a]
        to[0:ROWS, :] = own[c, p, a] + rows[c, p // 2, a]
        to[0:count, :] = to[0:count, :] + jnp.where(odd, close, distant)
        to[ROWS - count : ROWS, :] = to[ROWS - count : ROWS, :] + jnp.where(odd, distant, close)
    parts = []
    for a in range(BLOCKS):
        for c in range(3):
            parts.append(jnp.concatenate([total[c, p, a, 0:ROWS, :] for p in range(4)], axis=1))
    natural = placed(jnp.concatenate(parts, axis=0), matrix[...])
    for a in range(BLOCKS):
        for c in range(3):
            base = (a * 3 + c) * ROWS
            out[c, :, a * 512 : (a + 1) * 512] = natural[base : base + ROWS]


def final_kernel(base_end, second, third, fourth, matrix, out, rows, staged, sems):
    parts = []
    for a in range(BLOCKS):
        for c in range(3):
            pair = []
            for p in range(2):
                pair.append(second[c, p, a] + (third[c, p, a] + fourth[c, p, a]))
            parts.append(jnp.concatenate(pair, axis=1))
    spread = placed(jnp.concatenate(parts, axis=0), matrix[...])
    copies = []
    for a in range(BLOCKS):
        for c in range(3):
            base = (a * 3 + c) * 8
            for s in range(4):
                value = spread[base : base + 8, s * LANES : (s + 1) * LANES]
                rows[c, a * 4 + s, pl.ds(0, 8, stride=2), :] = value
                rows[c, a * 4 + s, pl.ds(1, 8, stride=2), :] = value
        for c in range(3):
            for s in range(4 * a, 4 * a + 4):
                cols = slice(s * LANES, (s + 1) * LANES)
                staged[c, :, cols] = base_end[c, :, cols] + rows[c, s]
        block = pl.ds(a * 512, 512)
        copies.append(pltpu.make_async_copy(staged.at[:, :, block], out.at[:, :, block], sems.at[a]))
        copies[-1].start()
    for copy in copies:
        copy.wait()


def f32(*shape):
    return jax.ShapeDtypeStruct(shape, jnp.float32)


def scratch(*shape):
    return pltpu.VMEM(shape, jnp.float32)


VMEM_SPEC = pl.BlockSpec(memory_space=pltpu.VMEM)
HBM_SPEC = pl.BlockSpec(memory_space=pltpu.HBM)


def in_hbm(array):
    return pltpu.with_memory_space_constraint(array, pltpu.HBM)


def call(kernel, ins, outs, scratches=(), name=None, cost=None):
    return pl.pallas_call(
        kernel,
        in_specs=[HBM_SPEC if own else VMEM_SPEC for own in ins],
        out_shape=[shape for shape, _ in outs],
        out_specs=[HBM_SPEC if own else VMEM_SPEC for _, own in outs],
        scratch_shapes=scratches,
        name=name,
        cost_estimate=cost,
        compiler_params=pltpu.CompilerParams(vmem_limit_bytes=VMEM_LIMIT),
    )


def per_device(start_states):
    tiles = lax.axis_size("tile")
    far_pairs = [(i, j) for k in range(1, tiles - 1, 2) for i, j in ((k, k + 1), (k + 1, k))]
    near_pairs = [(i, i ^ 1) for i in range(tiles)]
    dma = pltpu.SemaphoreType.DMA

    def bf16(array):
        return jax.ShapeDtypeStruct(array.shape, jnp.bfloat16)

    def here(array):
        return pltpu.VMEM(array.shape, array.dtype)

    coarse = (f32(3, 2, BLOCKS, 8, LANES), False)
    spilt = (f32(16 * SPILL_ROWS + SPARE, LANES), False)
    far_rows = (f32(FAR_ROWS + SPARE, LANES), False)
    last_rows = (f32(NEXT_ROWS + 16 * SPILL_ROWS + SPARE, LANES), False)
    fetched = (start_states[0], FINE_INVERSE, FINE_TABLE, COARSE_INVERSE, COARSE_TABLE)
    wide_end, propagated, u_wide, u_far, u_near, coarse_inverse = call(
        fine_kernel,
        [True] * 5,
        [
            (f32(3, 4, BLOCKS, 40, LANES), False),
            (f32(3, 2, BLOCKS, 16, LANES), False),
            (f32(3, 2, BLOCKS, 24, LANES), False),
            far_rows,
            far_rows,
            (bf16(COARSE_INVERSE), False),
        ],
        [
            scratch(3, ROWS, NX),
            pltpu.VMEM((512, 512), jnp.bfloat16),
            here(FINE_INVERSE),
            here(FINE_TABLE),
            here(COARSE_TABLE),
            dma((5,)),
            scratch(4, BLOCKS, 48, LANES),
            scratch(4, BLOCKS, 48, LANES),
            scratch(2, 4, BLOCKS, 48, LANES),
            scratch(2, 4, BLOCKS, 48, LANES),
            scratch(2, BLOCKS, 32, LANES),
            scratch(2, BLOCKS, 32, LANES),
            scratch(2, 2, BLOCKS, 32, LANES),
            scratch(2, 2, BLOCKS, 32, LANES),
        ],
        name="fine",
    )(*[in_hbm(array) for array in fetched])
    u_near = lax.ppermute(u_near, "tile", near_pairs)
    (u_far,) = call(join_kernel, [False] * 2, [far_rows], name="join")(u_far, u_near)
    own, spill_far, spill_near = call(
        spill_kernel,
        [False] * 3,
        [(f32(3, 4, BLOCKS, ROWS, LANES), False), spilt, spilt],
        [scratch(3, 2, BLOCKS, 32, LANES)],
        name="spill",
    )(wide_end, propagated, u_far)
    u_far = lax.ppermute(u_far, "tile", far_pairs)
    spill_far = lax.ppermute(spill_far, "tile", far_pairs)
    (near,) = call(forward_kernel, [False] * 2, [last_rows], name="forward")(u_far, spill_near)
    near = lax.ppermute(near, "tile", near_pairs)

    state = [
        scratch(2, BLOCKS, 48, LANES),
        scratch(2, BLOCKS, 48, LANES),
        scratch(2, 2, BLOCKS, 48, LANES),
        scratch(2, 2, BLOCKS, 48, LANES),
    ]
    (assembled,) = call(
        assemble_kernel,
        [False] * 3,
        [(f32(3, 2, BLOCKS, 48, LANES), False)],
        name="assemble",
        cost=pl.CostEstimate(flops=COST, bytes_accessed=COST // 100, transcendentals=0),
    )(u_wide, u_far, u_near)
    one, wide = call(
        first_kernel, [False] * 4, [coarse, (f32(3, 2, BLOCKS, 24, LANES), False)], state, name="first"
    )(assembled, near, coarse_inverse, COARSE_TABLE)
    early, two, mixed, last = call(rest_kernel, [False] * 4, [coarse] * 4, state, name="rest")(
        wide, one, coarse_inverse, COARSE_TABLE
    )
    first = lax.ppermute(early, "cuts", [(0, 1)])
    second = lax.ppermute(two, "cuts", [(0, 2), (1, 3)])
    third = lax.ppermute(mixed, "cuts", [(0, 3), (1, 2)])
    fourth = lax.ppermute(last, "cuts", [(2, 3)])
    (natural,) = call(
        natural_kernel,
        [False] * 5,
        [(f32(3, ROWS, NX), False)],
        [scratch(3, 2, BLOCKS, ROWS, LANES), scratch(3, 4, BLOCKS, ROWS + SPARE, LANES)],
        name="natural",
    )(own, spill_far, near, first, NATURAL)
    (out,) = call(
        final_kernel,
        [False] * 5,
        [(f32(3, ROWS, NX), True)],
        [scratch(3, 16, ROWS, LANES), scratch(3, ROWS, NX), dma((BLOCKS,))],
        name="final",
    )(natural, second, third, fourth, SPREAD)
    return out[None]


def solution(mesh):
    spec = P("cuts", None, "tile", None)
    return jax.shard_map(per_device, mesh=mesh, in_specs=(spec,), out_specs=spec, check_vma=False)
```

```python
import jax
import jax.numpy as jnp
import ml_dtypes
import numpy as np
from jax import lax
from jax.experimental import pallas as pl
from jax.experimental.pallas import tpu as pltpu
from jax.sharding import PartitionSpec as P

STEPS = 3
FINE_SPACING = 0.05
COARSE_SPACING = 0.1
FINE_STEP = 0.015
COARSE_STEP = 0.045

NX = 2048
ROWS = 16
UNKNOWNS = 512
BLOCKS = 4
LANES = 128
COST = 10**10
VMEM_LIMIT = 48 * 1024 * 1024


def halves(values):
    high = values.astype(np.float32).astype(ml_dtypes.bfloat16)
    low = (values - high.astype(np.float64)).astype(np.float32).astype(ml_dtypes.bfloat16)
    return high, low


def shifted(values):
    return np.concatenate([[0.0], values[:-1]])


def eliminated(lower, middle, upper):
    lower_e, lower_o = lower[0::2], lower[1::2]
    middle_e, middle_o = middle[0::2], middle[1::2]
    upper_e, upper_o = upper[0::2], upper[1::2]
    middle_n = np.append(middle_e[1:], 1.0)
    lower_n = np.append(lower_e[1:], 0.0)
    upper_n = np.append(upper_e[1:], 0.0)
    alpha = -lower_o / middle_e
    gamma = -upper_o / middle_n
    reduced = (alpha * lower_e, middle_o + alpha * upper_e + gamma * lower_n, gamma * upper_n)
    return alpha, gamma, reduced


def operator_tables(phases, columns, spacing, time_step):
    stride = NX // columns
    centers = (np.arange(columns) + 0.5) * stride
    depth = 0.9 + 0.3 * np.sin(6.0 * np.pi * centers / NX)
    beta = depth * depth / 3.0
    coupling = beta / (spacing * spacing)
    lower = -coupling.copy()
    lower[0] = 0.0
    upper = -coupling.copy()
    upper[-1] = 0.0
    middle = 1.0 + 2.0 * coupling
    slope = time_step * depth / (2.0 * spacing)
    weight = beta / (spacing * spacing + 4.0 * beta)
    rows = {}
    for p in range(phases):
        rows["slope", p] = slope[p::phases]
        rows["weight", p] = weight[p::phases]
        rows["centre", p] = 1.0 - 2.0 * weight[p::phases]
    alpha, gamma, first = eliminated(lower, middle, upper)
    if phases == 4:
        alpha2, gamma2, last = eliminated(*first)
        a1, a3, g1, g3 = alpha[0::2], alpha[1::2], gamma[0::2], gamma[1::2]
        rows["s0"] = alpha2 * a1
        rows["s1"] = alpha2
        rows["s2"] = a3 + alpha2 * g1
        rows["n1"] = shifted(gamma2)
        rows["n0"] = shifted(gamma2) * a1 + shifted(g3)
        rows["n2"] = shifted(gamma2) * g1
        l1, m1, u1 = (v[0::2] for v in first)
        rows["b1"] = 1.0 / m1
        rows["b0"] = a1 / m1
        rows["b2"] = g1 / m1
        rows["bp"] = -l1 / m1
        rows["b3"] = -u1 / m1
        rows["c0"] = 1.0 / middle[0::4]
        rows["cp"] = -lower[0::4] / middle[0::4]
        rows["c1"] = -upper[0::4] / middle[0::4]
        rows["d2"] = 1.0 / middle[2::4]
        rows["d1"] = -lower[2::4] / middle[2::4]
        rows["d3"] = -upper[2::4] / middle[2::4]
    else:
        last = first
        rows["s0"] = alpha
        rows["n0"] = shifted(gamma)
        rows["c0"] = 1.0 / middle[0::2]
        rows["cp"] = -lower[0::2] / middle[0::2]
        rows["c1"] = -upper[0::2] / middle[0::2]
    low, mid, up = last
    matrix = np.diag(mid) + np.diag(low[1:], -1) + np.diag(up[:-1], 1)
    inverse = np.linalg.inv(matrix)
    names = {name: i for i, name in enumerate(rows)}
    table = np.stack(list(rows.values())).reshape(-1, LANES).astype(np.float32)
    return names, table, np.stack(halves(inverse.T))


FINE_NAMES, FINE_TABLE, FINE_INVERSE = operator_tables(4, NX, FINE_SPACING, FINE_STEP)
COARSE_NAMES, COARSE_TABLE, COARSE_INVERSE = operator_tables(2, NX // 2, COARSE_SPACING, COARSE_STEP)


def phase_matrix():
    matrix = np.zeros((512, 512), np.float32)
    j = np.arange(512)
    matrix[j, (j % 4) * LANES + j // 4] = 1.0
    return matrix


NATURAL = phase_matrix().T.copy().astype(ml_dtypes.bfloat16)


def spread_matrix():
    matrix = np.zeros((256, 512), np.float32)
    c = np.arange(512)
    coarse = c // 2
    matrix[(coarse % 2) * LANES + coarse // 2, c] = 1.0
    return matrix


SPREAD = spread_matrix().astype(ml_dtypes.bfloat16)


def split(values):
    high = values.astype(jnp.bfloat16)
    low = (values - high.astype(jnp.float32)).astype(jnp.bfloat16)
    return high, low


def dot(a, b):
    return jnp.dot(a, b, preferred_element_type=jnp.float32)


def placed(values, matrix):
    count = values.shape[0]
    high, low = split(values)
    both = dot(jnp.concatenate([high, low], axis=0), matrix)
    return both[:count] + both[count:]


def lane_index(rows):
    return lax.broadcasted_iota(jnp.int32, (rows, LANES), 1)


def following(tiles):
    lane = lane_index(tiles[0].shape[0])
    rolled = [pltpu.roll(t, LANES - 1, 1) for t in tiles] + [jnp.zeros_like(tiles[0])]
    return [jnp.where(lane == LANES - 1, rolled[a + 1], rolled[a]) for a in range(BLOCKS)]


def preceding(tiles):
    lane = lane_index(tiles[0].shape[0])
    rolled = [jnp.zeros_like(tiles[0])] + [pltpu.roll(t, 1, 1) for t in tiles]
    return [jnp.where(lane == 0, rolled[a], rolled[a + 1]) for a in range(BLOCKS)]


def inside(first, count, total):
    row = lax.broadcasted_iota(jnp.int32, (count, LANES), 0) + first
    return jnp.where((row >= 0) & (row < total), 1.0, 0.0).astype(jnp.float32)


def step_stages(phases, names, table, inverse, ratio, height, height_new, flux, diff, windows, origin, total):
    (h0, hn), (d0, dn), ends = windows
    last = phases - 1

    def coef(name, a):
        i = names[name] * BLOCKS + a
        return table[i : i + 1, :]

    mask = inside(origin + h0, hn, total)
    rows = pl.ds(h0, hn)
    before = preceding([flux[0, last, a, rows, :] for a in range(BLOCKS)])
    after = following([flux[0, 0, a, rows, :] for a in range(BLOCKS)])
    for p in range(phases):
        for a in range(BLOCKS):
            right = after[a] if p == last else flux[0, p + 1, a, rows, :]
            left = before[a] if p == 0 else flux[0, p - 1, a, rows, :]
            down = flux[1, p, a, pl.ds(h0 + 1, hn), :]
            upper = flux[1, p, a, pl.ds(h0 - 1, hn), :]
            change = (right - left) + (down - upper)
            height_new[p, a, rows, :] = (height[p, a, rows, :] - ratio * change) * mask
    yield

    rows = pl.ds(d0, dn)
    mask = inside(origin + d0, dn, total)

    def reduce(i):
        if i == 0:
            before = preceding([height_new[last, a, rows, :] for a in range(BLOCKS)])
            after = following([height_new[0, a, rows, :] for a in range(BLOCKS)])
        own, passed = [], []
        for a in range(BLOCKS):
            force = []
            for p in range(phases):
                if i == 0:
                    right = after[a] if p == last else height_new[p + 1, a, rows, :]
                    left = before[a] if p == 0 else height_new[p - 1, a, rows, :]
                    value = flux[0, p, a, rows, :] - coef(("slope", p), a) * (right - left)
                else:
                    down = height_new[p, a, pl.ds(d0 + 1, dn), :]
                    upper = height_new[p, a, pl.ds(d0 - 1, dn), :]
                    value = (flux[1, p, a, rows, :] - coef(("slope", p), a) * (down - upper)) * mask
                if p < last:
                    diff[i, p, a, rows, :] = value
                force.append(value)
            kept = force[last] + coef("s0", a) * force[0]
            sent = coef("n0", a) * force[0]
            if phases == 4:
                kept = kept + coef("s1", a) * force[1] + coef("s2", a) * force[2]
                sent = sent + coef("n1", a) * force[1] + coef("n2", a) * force[2]
            own.append(kept)
            passed.append(sent)
        arrived = following(passed)
        return jnp.concatenate([own[a] + arrived[a] for a in range(BLOCKS)], axis=1)

    def expand(i, solved):
        ends = [solved[:, a * LANES : (a + 1) * LANES] for a in range(BLOCKS)]
        before = preceding(ends)
        for a in range(BLOCKS):
            end, prior = ends[a], before[a]
            f0 = diff[i, 0, a, rows, :]
            if phases == 4:
                f1 = diff[i, 1, a, rows, :]
                f2 = diff[i, 2, a, rows, :]
                x1 = (
                    coef("b1", a) * f1
                    + coef("b0", a) * f0
                    + coef("b2", a) * f2
                    + coef("bp", a) * prior
                    + coef("b3", a) * end
                )
                x0 = coef("c0", a) * f0 + coef("cp", a) * prior + coef("c1", a) * x1
                x2 = coef("d2", a) * f2 + coef("d1", a) * x1 + coef("d3", a) * end
                trial = [x0, x1, x2, end]
            else:
                trial = [coef("c0", a) * f0 + coef("cp", a) * prior + coef("c1", a) * end, end]
            for p in range(phases):
                diff[i, p, a, rows, :] = trial[p] - flux[i, p, a, rows, :]

    pair = [reduce(0), reduce(1)]
    yield
    solved = solve(jnp.concatenate(pair, axis=0), inverse)
    yield
    expand(0, solved[:dn])
    expand(1, solved[dn:])
    yield

    for i in range(2):
        o0, on = ends[i]
        mask = inside(origin + o0, on, total)
        rows = pl.ds(o0, on)
        for p in range(phases):
            for a in range(BLOCKS):
                middle = diff[i, p, a, rows, :]
                down = diff[i, p, a, pl.ds(o0 + 1, on), :]
                upper = diff[i, p, a, pl.ds(o0 - 1, on), :]
                sides = coef(("weight", p), a) * (down + upper)
                flux[i, p, a, rows, :] = (flux[i, p, a, rows, :] + coef(("centre", p), a) * middle + sides) * mask
    yield


def solve(right, inverse):
    count = right.shape[0]
    high, low = split(right)
    both = dot(jnp.concatenate([high, low], axis=0), inverse[0])
    return both[:count] + both[count:] + dot(high, inverse[1])


def wave_step(*arguments):
    for _ in step_stages(*arguments):
        pass


FINE_RATIO = FINE_STEP / (2.0 * FINE_SPACING)
COARSE_RATIO = COARSE_STEP / (2.0 * COARSE_SPACING)


def on_odd():
    return lax.rem(lax.axis_index("tile"), 2) == 1


def planes(phases):
    return [(c, p, a) for c in range(3) for p in range(phases) for a in range(BLOCKS)]


SPILL = ((0, 8), (8, 8), (16, 9))
SPILL_ROWS = 25
FAR_ROWS = 24 * 14
NEXT_ROWS = 24 * 6
SPARE = 8


def fetch(pairs, sems):
    copies = [pltpu.make_async_copy(source, target, sems.at[i]) for i, (source, target) in enumerate(pairs)]
    for copy in copies:
        copy.start()
    return copies


def at_tile(tile_rows, offset):
    return lax.axis_index("tile") * tile_rows - offset, lax.axis_size("tile") * tile_rows


def fine_kernel(
    x_hbm, fine_inverse_hbm, fine_table_hbm, coarse_inverse_hbm, coarse_table_hbm,
    wide_end, propagated, u_wide, u_far, u_near, coarse_inverse,
    x, matrix, fine_inverse, fine_table, coarse_table, sems,
    height, height_new, flux, diff, c_height, c_height_new, c_flux, c_diff,
):
    copies = fetch(
        (
            (x_hbm, x),
            (fine_table_hbm, fine_table),
            (coarse_table_hbm, coarse_table),
            (fine_inverse_hbm, fine_inverse),
            (coarse_inverse_hbm, coarse_inverse),
        ),
        sems,
    )
    for ref in (height, height_new, flux, diff):
        for edge in (pl.ds(0, 16), pl.ds(32, 16)):
            target = ref.at[..., edge, :]
            target[...] = jnp.zeros(target.shape, jnp.float32)
    for ref in (c_height, c_height_new, c_flux, c_diff):
        ref[...] = jnp.zeros(ref.shape, jnp.float32)
    row = lax.broadcasted_iota(jnp.int32, (512, 512), 0)
    column = lax.broadcasted_iota(jnp.int32, (512, 512), 1)
    chosen = column == (row & 3) * LANES + (row >> 2)
    matrix[...] = jnp.where(chosen, 1.0, 0.0).astype(jnp.bfloat16)
    copies[0].wait()

    parts = []
    for a in range(BLOCKS):
        for c in range(3):
            parts.append(x[c, :, a * 512 : (a + 1) * 512])
    phased = placed(jnp.concatenate(parts, axis=0), matrix[...])
    for c, p, a in planes(4):
        to = height.at[p, a] if c == 0 else flux.at[c - 1, p, a]
        base = (a * 3 + c) * ROWS
        to[16:32, :] = phased[base : base + ROWS, p * LANES : (p + 1) * LANES]

    def restricted(ref, p, a, first, count):
        total = None
        for q in (2 * p, 2 * p + 1):
            for r in (first, first + 1):
                part = ref(q, a)[pl.ds(r, count, stride=2), :]
                total = part if total is None else total + part
        return 0.25 * total

    for p in range(2):
        for a in range(BLOCKS):
            c_height[p, a, 12:20, :] = restricted(lambda q, b: height.at[q, b], p, a, 16, 8)
            for i in range(2):
                c_flux[i, p, a, 12:20, :] = restricted(lambda q, b: flux.at[i, q, b], p, a, 16, 8)
    for copy in copies[1:3]:
        copy.wait()

    coarse_arguments = (
        2, COARSE_NAMES, coarse_table, coarse_inverse, COARSE_RATIO, c_height, c_height_new, c_flux, c_diff,
        ((8, 16), (8, 16), ((8, 16), (8, 16))), *at_tile(ROWS // 2, 12),
    )
    fine_arguments = (4, FINE_NAMES, fine_table, fine_inverse, FINE_RATIO)
    place = at_tile(ROWS, 16)
    windows = ((12, 24), (12, 24), ((12, 24), (12, 24)))
    stages = (
        step_stages(*fine_arguments, height, height_new, flux, diff, windows, *place),
        step_stages(*coarse_arguments),
    )
    for _ in range(2):
        for stage in stages:
            next(stage)
    for copy in copies[3:]:
        copy.wait()
    for _ in zip(*stages):
        pass
    wave_step(*fine_arguments, height_new, height, flux, diff, ((12, 24), (8, 32), ((8, 32), (8, 32))), *place)
    wave_step(*fine_arguments, height, height_new, flux, diff, ((8, 32), (8, 32), ((8, 32), (4, 40))), *place)

    odd = on_odd()
    later = jnp.where(lax.axis_index("cuts") > 0, 1.0, 0.0).astype(jnp.float32)
    for n, (c, p, a) in enumerate(planes(2)):
        if c == 0:
            end = restricted(lambda q, b: height_new.at[q, b], p, a, 0, 24)
            step = c_height_new[p, a, 4:28, :]
        else:
            end = restricted(lambda q, b: flux.at[c - 1, q, b], p, a, 0, 24)
            step = c_flux[c - 1, p, a, 4:28, :]
        step = later * step
        propagated[c, p, a] = step[4:20]
        u = end - step
        u_wide[c, p, a] = u
        c_diff[0, p, a, 4:28, :] = u
        to_next = c_diff[0, p, a, 11:25, :]
        to_previous = c_diff[0, p, a, 7:21, :]
        u_far[n * 14 : n * 14 + 14, :] = jnp.where(odd, to_next, to_previous)
        u_near[n * 14 : n * 14 + 14, :] = jnp.where(odd, to_previous, to_next)
    for c, p, a in planes(4):
        source = height_new.at[p, a] if c == 0 else flux.at[c - 1, p, a]
        wide_end[c, p, a] = source[4:44, :]


def spill_kernel(wide_end, propagated, arrived, own, to_far, to_near, rows):
    del arrived
    odd = on_odd()
    for c, p, a in planes(2):
        value = propagated[c, p, a]
        rows[c, p, a, pl.ds(0, 16, stride=2), :] = value
        rows[c, p, a, pl.ds(1, 16, stride=2), :] = value
    for c, p, a in planes(4):
        start, count = SPILL[c]
        base = (p * BLOCKS + a) * SPILL_ROWS + start
        wide_end[c, p, a, 4:36, :] = wide_end[c, p, a, 4:36, :] - rows[c, p // 2, a]
        own[c, p, a] = wide_end[c, p, a, 12:28, :]
        to_next = wide_end[c, p, a, 28 : 28 + count, :]
        to_previous = wide_end[c, p, a, 12 - count : 12, :]
        to_far[base : base + count, :] = jnp.where(odd, to_next, to_previous)
        to_near[base : base + count, :] = jnp.where(odd, to_previous, to_next)


def join_kernel(own, near, out):
    odd = on_odd()

    @pl.when(odd)
    def _():
        for n in range(24):
            base = n * 14
            out[base + 6 : base + 14, :] = own[base + 6 : base + 14, :]
            out[base : base + 6, :] = own[base : base + 6, :] + near[base + 8 : base + 14, :]

    @pl.when(jnp.logical_not(odd))
    def _():
        for n in range(24):
            base = n * 14
            out[base : base + 8, :] = own[base : base + 8, :]
            out[base + 8 : base + 14, :] = own[base + 8 : base + 14, :] + near[base : base + 6, :]


def forward_kernel(far, rows, out):
    odd = on_odd()
    for n in range(24):
        low = far[n * 14 : n * 14 + 6, :]
        high = far[n * 14 + 8 : n * 14 + 14, :]
        out[n * 6 : n * 6 + 6, :] = jnp.where(odd, low, high)
    out[NEXT_ROWS : NEXT_ROWS + 16 * SPILL_ROWS, :] = rows[0 : 16 * SPILL_ROWS, :]


def assemble_kernel(own, far, near, out):
    odd = on_odd()
    for n, (c, p, a) in enumerate(planes(2)):
        to = out.at[c, p, a]
        distant = far[n * 14 : n * 14 + 14, :]
        close = near[n * 14 : n * 14 + 14, :]
        to[0:8, :] = jnp.zeros((8, LANES), jnp.float32)
        to[8:32, :] = own[c, p, a]
        to[32:40, :] = jnp.zeros((8, LANES), jnp.float32)
        to[7:21, :] = to[7:21, :] + jnp.where(odd, close, distant)
        to[19:33, :] = to[19:33, :] + jnp.where(odd, distant, close)


def first_kernel(assembled, cross, inverse, table, one, wide, height, height_new, flux, diff):
    odd = on_odd()

    @pl.when(lax.axis_index("cuts") < lax.axis_size("cuts") - 1)
    def _():
        for n, (c, p, a) in enumerate(planes(2)):
            to = height.at[p, a] if c == 0 else flux.at[c - 1, p, a]
            beyond = cross[n * 6 : n * 6 + 6, :]
            to[0:40, :] = assembled[c, p, a, 0:40, :]
            to[7:13, :] = to[7:13, :] + jnp.where(odd, beyond, 0.0)
            to[27:33, :] = to[27:33, :] + jnp.where(odd, 0.0, beyond)
        window = (8, 24)
        wave_step(
            2, COARSE_NAMES, table, inverse, COARSE_RATIO, height, height_new, flux, diff,
            (window, window, (window, window)), *at_tile(ROWS // 2, 16),
        )
        for c, p, a in planes(2):
            result = height_new.at[p, a] if c == 0 else flux.at[c - 1, p, a]
            one[c, p, a] = result[16:24, :]
            wide[c, p, a] = result[8:32, :]


def rest_kernel(wide, one, inverse, table, early, two, three, last, height, height_new, flux, diff):
    cut = lax.axis_index("cuts")
    arguments = (2, COARSE_NAMES, table, inverse, COARSE_RATIO)
    for c, p, a in planes(2):
        early[c, p, a] = one[c, p, a]
        last[c, p, a] = one[c, p, a]

    @pl.when(cut < 2)
    def _():
        for c, p, a in planes(2):
            to = height.at[p, a] if c == 0 else flux.at[c - 1, p, a]
            to[8:32, :] = wide[c, p, a]
        windows = ((8, 24), (12, 16), ((12, 16), (12, 16)))
        wave_step(*arguments, height, height_new, flux, diff, windows, *at_tile(ROWS // 2, 16))
        for c, p, a in planes(2):
            result = height_new.at[p, a] if c == 0 else flux.at[c - 1, p, a]
            two[c, p, a] = result[16:24, :]

    @pl.when(cut == 0)
    def _():
        windows = ((12, 16), (12, 16), ((16, 8), (16, 8)))
        wave_step(*arguments, height_new, height, flux, diff, windows, *at_tile(ROWS // 2, 16))
        for c, p, a in planes(2):
            result = height.at[p, a] if c == 0 else flux.at[c - 1, p, a]
            three[c, p, a] = result[16:24, :]


def natural_kernel(own, far, near, first, matrix, out, rows, total):
    odd = on_odd()
    for c, p, a in planes(2):
        rows[c, p, a, pl.ds(0, 8, stride=2), :] = first[c, p, a]
        rows[c, p, a, pl.ds(1, 8, stride=2), :] = first[c, p, a]
    for c, p, a in planes(4):
        start, count = SPILL[c]
        base = (p * BLOCKS + a) * SPILL_ROWS + start
        distant = far[base : base + count, :]
        close = near[NEXT_ROWS + base : NEXT_ROWS + base + count, :]
        to = total.at[c, p, a]
        to[0:ROWS, :] = own[c, p, a] + rows[c, p // 2, a]
        to[0:count, :] = to[0:count, :] + jnp.where(odd, close, distant)
        to[ROWS - count : ROWS, :] = to[ROWS - count : ROWS, :] + jnp.where(odd, distant, close)
    parts = []
    for a in range(BLOCKS):
        for c in range(3):
            parts.append(jnp.concatenate([total[c, p, a, 0:ROWS, :] for p in range(4)], axis=1))
    natural = placed(jnp.concatenate(parts, axis=0), matrix[...])
    for a in range(BLOCKS):
        for c in range(3):
            base = (a * 3 + c) * ROWS
            out[c, :, a * 512 : (a + 1) * 512] = natural[base : base + ROWS]


def final_kernel(base_end, second, third, fourth, matrix, out, rows, staged, sems):
    parts = []
    for a in range(BLOCKS):
        for c in range(3):
            pair = []
            for p in range(2):
                pair.append(second[c, p, a] + (third[c, p, a] + fourth[c, p, a]))
            parts.append(jnp.concatenate(pair, axis=1))
    spread = placed(jnp.concatenate(parts, axis=0), matrix[...])
    copies = []
    for a in range(BLOCKS):
        for c in range(3):
            base = (a * 3 + c) * 8
            for s in range(4):
                value = spread[base : base + 8, s * LANES : (s + 1) * LANES]
                rows[c, a * 4 + s, pl.ds(0, 8, stride=2), :] = value
                rows[c, a * 4 + s, pl.ds(1, 8, stride=2), :] = value
        for c in range(3):
            for s in range(4 * a, 4 * a + 4):
                cols = slice(s * LANES, (s + 1) * LANES)
                staged[c, :, cols] = base_end[c, :, cols] + rows[c, s]
        block = pl.ds(a * 512, 512)
        copies.append(pltpu.make_async_copy(staged.at[:, :, block], out.at[:, :, block], sems.at[a]))
        copies[-1].start()
    for copy in copies:
        copy.wait()


def f32(*shape):
    return jax.ShapeDtypeStruct(shape, jnp.float32)


def scratch(*shape):
    return pltpu.VMEM(shape, jnp.float32)


VMEM_SPEC = pl.BlockSpec(memory_space=pltpu.VMEM)
HBM_SPEC = pl.BlockSpec(memory_space=pltpu.HBM)


def in_hbm(array):
    return pltpu.with_memory_space_constraint(array, pltpu.HBM)


def call(kernel, ins, outs, scratches=(), name=None, cost=None):
    return pl.pallas_call(
        kernel,
        in_specs=[HBM_SPEC if own else VMEM_SPEC for own in ins],
        out_shape=[shape for shape, _ in outs],
        out_specs=[HBM_SPEC if own else VMEM_SPEC for _, own in outs],
        scratch_shapes=scratches,
        name=name,
        cost_estimate=cost,
        compiler_params=pltpu.CompilerParams(vmem_limit_bytes=VMEM_LIMIT),
    )


def per_device(start_states):
    tiles = lax.axis_size("tile")
    far_pairs = [(i, j) for k in range(1, tiles - 1, 2) for i, j in ((k, k + 1), (k + 1, k))]
    near_pairs = [(i, i ^ 1) for i in range(tiles)]
    dma = pltpu.SemaphoreType.DMA

    def bf16(array):
        return jax.ShapeDtypeStruct(array.shape, jnp.bfloat16)

    def here(array):
        return pltpu.VMEM(array.shape, array.dtype)

    coarse = (f32(3, 2, BLOCKS, 8, LANES), False)
    spilt = (f32(16 * SPILL_ROWS + SPARE, LANES), False)
    far_rows = (f32(FAR_ROWS + SPARE, LANES), False)
    last_rows = (f32(NEXT_ROWS + 16 * SPILL_ROWS + SPARE, LANES), False)
    fetched = (start_states[0], FINE_INVERSE, FINE_TABLE, COARSE_INVERSE, COARSE_TABLE)
    wide_end, propagated, u_wide, u_far, u_near, coarse_inverse = call(
        fine_kernel,
        [True] * 5,
        [
            (f32(3, 4, BLOCKS, 40, LANES), False),
            (f32(3, 2, BLOCKS, 16, LANES), False),
            (f32(3, 2, BLOCKS, 24, LANES), False),
            far_rows,
            far_rows,
            (bf16(COARSE_INVERSE), False),
        ],
        [
            scratch(3, ROWS, NX),
            pltpu.VMEM((512, 512), jnp.bfloat16),
            here(FINE_INVERSE),
            here(FINE_TABLE),
            here(COARSE_TABLE),
            dma((5,)),
            scratch(4, BLOCKS, 48, LANES),
            scratch(4, BLOCKS, 48, LANES),
            scratch(2, 4, BLOCKS, 48, LANES),
            scratch(2, 4, BLOCKS, 48, LANES),
            scratch(2, BLOCKS, 32, LANES),
            scratch(2, BLOCKS, 32, LANES),
            scratch(2, 2, BLOCKS, 32, LANES),
            scratch(2, 2, BLOCKS, 32, LANES),
        ],
        name="fine",
    )(*[in_hbm(array) for array in fetched])
    senders = range(lax.axis_size("cuts") - 1)

    def of_senders(pairs):
        return [(k * tiles + i, k * tiles + j) for k in senders for i, j in pairs]

    u_near = lax.ppermute(u_near, "tile", near_pairs)
    (u_far,) = call(join_kernel, [False] * 2, [far_rows], name="join")(u_far, u_near)
    own, spill_far, spill_near = call(
        spill_kernel,
        [False] * 3,
        [(f32(3, 4, BLOCKS, ROWS, LANES), False), spilt, spilt],
        [scratch(3, 2, BLOCKS, 32, LANES)],
        name="spill",
    )(wide_end, propagated, u_far)
    u_far = lax.ppermute(u_far, ("cuts", "tile"), of_senders(far_pairs))
    spill_far = lax.ppermute(spill_far, "tile", far_pairs)
    (near,) = call(forward_kernel, [False] * 2, [last_rows], name="forward")(u_far, spill_near)
    near = lax.ppermute(near, "tile", near_pairs)

    state = [
        scratch(2, BLOCKS, 48, LANES),
        scratch(2, BLOCKS, 48, LANES),
        scratch(2, 2, BLOCKS, 48, LANES),
        scratch(2, 2, BLOCKS, 48, LANES),
    ]
    (assembled,) = call(
        assemble_kernel,
        [False] * 3,
        [(f32(3, 2, BLOCKS, 48, LANES), False)],
        name="assemble",
        cost=pl.CostEstimate(flops=COST, bytes_accessed=COST // 100, transcendentals=0),
    )(u_wide, u_far, u_near)
    one, wide = call(
        first_kernel, [False] * 4, [coarse, (f32(3, 2, BLOCKS, 24, LANES), False)], state, name="first"
    )(assembled, near, coarse_inverse, COARSE_TABLE)
    early, two, three, last = call(rest_kernel, [False] * 4, [coarse] * 4, state, name="rest")(
        wide, one, coarse_inverse, COARSE_TABLE
    )
    first = lax.ppermute(early, "cuts", [(0, 1), (1, 2)])
    second = lax.ppermute(two, "cuts", [(0, 2), (1, 3)])
    third = lax.ppermute(three, "cuts", [(0, 3)])
    fourth = lax.ppermute(last, "cuts", [(2, 3)])
    (natural,) = call(
        natural_kernel,
        [False] * 5,
        [(f32(3, ROWS, NX), False)],
        [scratch(3, 2, BLOCKS, ROWS, LANES), scratch(3, 4, BLOCKS, ROWS + SPARE, LANES)],
        name="natural",
    )(own, spill_far, near, first, NATURAL)
    (out,) = call(
        final_kernel,
        [False] * 5,
        [(f32(3, ROWS, NX), True)],
        [scratch(3, 16, ROWS, LANES), scratch(3, ROWS, NX), dma((BLOCKS,))],
        name="final",
    )(natural, third, second, fourth, SPREAD)
    return out[None]


def solution(mesh):
    spec = P("cuts", None, "tile", None)
    return jax.shard_map(per_device, mesh=mesh, in_specs=(spec,), out_specs=spec, check_vma=False)
```

```python
import jax
import jax.numpy as jnp
import ml_dtypes
import numpy as np
from jax import lax
from jax.experimental import pallas as pl
from jax.experimental.pallas import tpu as pltpu
from jax.sharding import PartitionSpec as P

STEPS = 3
FINE_SPACING = 0.05
COARSE_SPACING = 0.1
FINE_STEP = 0.015
COARSE_STEP = 0.045

NX = 2048
ROWS = 16
UNKNOWNS = 512
BLOCKS = 4
LANES = 128
COST = 10**10
VMEM_LIMIT = 48 * 1024 * 1024


def halves(values):
    high = values.astype(np.float32).astype(ml_dtypes.bfloat16)
    low = (values - high.astype(np.float64)).astype(np.float32).astype(ml_dtypes.bfloat16)
    return high, low


def shifted(values):
    return np.concatenate([[0.0], values[:-1]])


def eliminated(lower, middle, upper):
    lower_e, lower_o = lower[0::2], lower[1::2]
    middle_e, middle_o = middle[0::2], middle[1::2]
    upper_e, upper_o = upper[0::2], upper[1::2]
    middle_n = np.append(middle_e[1:], 1.0)
    lower_n = np.append(lower_e[1:], 0.0)
    upper_n = np.append(upper_e[1:], 0.0)
    alpha = -lower_o / middle_e
    gamma = -upper_o / middle_n
    reduced = (alpha * lower_e, middle_o + alpha * upper_e + gamma * lower_n, gamma * upper_n)
    return alpha, gamma, reduced


def operator_tables(phases, columns, spacing, time_step):
    stride = NX // columns
    centers = (np.arange(columns) + 0.5) * stride
    depth = 0.9 + 0.3 * np.sin(6.0 * np.pi * centers / NX)
    beta = depth * depth / 3.0
    coupling = beta / (spacing * spacing)
    lower = -coupling.copy()
    lower[0] = 0.0
    upper = -coupling.copy()
    upper[-1] = 0.0
    middle = 1.0 + 2.0 * coupling
    slope = time_step * depth / (2.0 * spacing)
    weight = beta / (spacing * spacing + 4.0 * beta)
    rows = {}
    for p in range(phases):
        rows["slope", p] = slope[p::phases]
        rows["weight", p] = weight[p::phases]
        rows["centre", p] = 1.0 - 2.0 * weight[p::phases]
    alpha, gamma, first = eliminated(lower, middle, upper)
    if phases == 4:
        alpha2, gamma2, last = eliminated(*first)
        a1, a3, g1, g3 = alpha[0::2], alpha[1::2], gamma[0::2], gamma[1::2]
        rows["s0"] = alpha2 * a1
        rows["s1"] = alpha2
        rows["s2"] = a3 + alpha2 * g1
        rows["n1"] = shifted(gamma2)
        rows["n0"] = shifted(gamma2) * a1 + shifted(g3)
        rows["n2"] = shifted(gamma2) * g1
        l1, m1, u1 = (v[0::2] for v in first)
        rows["b1"] = 1.0 / m1
        rows["b0"] = a1 / m1
        rows["b2"] = g1 / m1
        rows["bp"] = -l1 / m1
        rows["b3"] = -u1 / m1
        rows["c0"] = 1.0 / middle[0::4]
        rows["cp"] = -lower[0::4] / middle[0::4]
        rows["c1"] = -upper[0::4] / middle[0::4]
        rows["d2"] = 1.0 / middle[2::4]
        rows["d1"] = -lower[2::4] / middle[2::4]
        rows["d3"] = -upper[2::4] / middle[2::4]
    else:
        last = first
        rows["s0"] = alpha
        rows["n0"] = shifted(gamma)
        rows["c0"] = 1.0 / middle[0::2]
        rows["cp"] = -lower[0::2] / middle[0::2]
        rows["c1"] = -upper[0::2] / middle[0::2]
    low, mid, up = last
    matrix = np.diag(mid) + np.diag(low[1:], -1) + np.diag(up[:-1], 1)
    inverse = np.linalg.inv(matrix)
    names = {name: i for i, name in enumerate(rows)}
    table = np.stack(list(rows.values())).reshape(-1, LANES).astype(np.float32)
    return names, table, np.stack(halves(inverse.T))


FINE_NAMES, FINE_TABLE, FINE_INVERSE = operator_tables(4, NX, FINE_SPACING, FINE_STEP)
COARSE_NAMES, COARSE_TABLE, COARSE_INVERSE = operator_tables(2, NX // 2, COARSE_SPACING, COARSE_STEP)


def phase_matrix():
    matrix = np.zeros((512, 512), np.float32)
    j = np.arange(512)
    matrix[j, (j % 4) * LANES + j // 4] = 1.0
    return matrix


NATURAL = phase_matrix().T.copy().astype(ml_dtypes.bfloat16)


def spread_matrix():
    matrix = np.zeros((256, 512), np.float32)
    c = np.arange(512)
    coarse = c // 2
    matrix[(coarse % 2) * LANES + coarse // 2, c] = 1.0
    return matrix


SPREAD = spread_matrix().astype(ml_dtypes.bfloat16)


def split(values):
    high = values.astype(jnp.bfloat16)
    low = (values - high.astype(jnp.float32)).astype(jnp.bfloat16)
    return high, low


def dot(a, b):
    return jnp.dot(a, b, preferred_element_type=jnp.float32)


def placed(values, matrix):
    count = values.shape[0]
    high, low = split(values)
    both = dot(jnp.concatenate([high, low], axis=0), matrix)
    return both[:count] + both[count:]


def lane_index(rows):
    return lax.broadcasted_iota(jnp.int32, (rows, LANES), 1)


def following(tiles):
    lane = lane_index(tiles[0].shape[0])
    rolled = [pltpu.roll(t, LANES - 1, 1) for t in tiles] + [jnp.zeros_like(tiles[0])]
    return [jnp.where(lane == LANES - 1, rolled[a + 1], rolled[a]) for a in range(BLOCKS)]


def preceding(tiles):
    lane = lane_index(tiles[0].shape[0])
    rolled = [jnp.zeros_like(tiles[0])] + [pltpu.roll(t, 1, 1) for t in tiles]
    return [jnp.where(lane == 0, rolled[a], rolled[a + 1]) for a in range(BLOCKS)]


def inside(first, count, total):
    row = lax.broadcasted_iota(jnp.int32, (count, LANES), 0) + first
    return jnp.where((row >= 0) & (row < total), 1.0, 0.0).astype(jnp.float32)


def step_stages(phases, names, table, inverse, ratio, height, height_new, flux, diff, windows, origin, total):
    (h0, hn), (d0, dn), ends = windows
    last = phases - 1

    def coef(name, a):
        i = names[name] * BLOCKS + a
        return table[i : i + 1, :]

    mask = inside(origin + h0, hn, total)
    rows = pl.ds(h0, hn)
    before = preceding([flux[0, last, a, rows, :] for a in range(BLOCKS)])
    after = following([flux[0, 0, a, rows, :] for a in range(BLOCKS)])
    for p in range(phases):
        for a in range(BLOCKS):
            right = after[a] if p == last else flux[0, p + 1, a, rows, :]
            left = before[a] if p == 0 else flux[0, p - 1, a, rows, :]
            down = flux[1, p, a, pl.ds(h0 + 1, hn), :]
            upper = flux[1, p, a, pl.ds(h0 - 1, hn), :]
            change = (right - left) + (down - upper)
            height_new[p, a, rows, :] = (height[p, a, rows, :] - ratio * change) * mask
    yield

    rows = pl.ds(d0, dn)
    mask = inside(origin + d0, dn, total)

    def reduce(i):
        if i == 0:
            before = preceding([height_new[last, a, rows, :] for a in range(BLOCKS)])
            after = following([height_new[0, a, rows, :] for a in range(BLOCKS)])
        own, passed = [], []
        for a in range(BLOCKS):
            force = []
            for p in range(phases):
                if i == 0:
                    right = after[a] if p == last else height_new[p + 1, a, rows, :]
                    left = before[a] if p == 0 else height_new[p - 1, a, rows, :]
                    value = flux[0, p, a, rows, :] - coef(("slope", p), a) * (right - left)
                else:
                    down = height_new[p, a, pl.ds(d0 + 1, dn), :]
                    upper = height_new[p, a, pl.ds(d0 - 1, dn), :]
                    value = (flux[1, p, a, rows, :] - coef(("slope", p), a) * (down - upper)) * mask
                if p < last:
                    diff[i, p, a, rows, :] = value
                force.append(value)
            kept = force[last] + coef("s0", a) * force[0]
            sent = coef("n0", a) * force[0]
            if phases == 4:
                kept = kept + coef("s1", a) * force[1] + coef("s2", a) * force[2]
                sent = sent + coef("n1", a) * force[1] + coef("n2", a) * force[2]
            own.append(kept)
            passed.append(sent)
        arrived = following(passed)
        return jnp.concatenate([own[a] + arrived[a] for a in range(BLOCKS)], axis=1)

    def expand(i, solved):
        ends = [solved[:, a * LANES : (a + 1) * LANES] for a in range(BLOCKS)]
        before = preceding(ends)
        for a in range(BLOCKS):
            end, prior = ends[a], before[a]
            f0 = diff[i, 0, a, rows, :]
            if phases == 4:
                f1 = diff[i, 1, a, rows, :]
                f2 = diff[i, 2, a, rows, :]
                x1 = (
                    coef("b1", a) * f1
                    + coef("b0", a) * f0
                    + coef("b2", a) * f2
                    + coef("bp", a) * prior
                    + coef("b3", a) * end
                )
                x0 = coef("c0", a) * f0 + coef("cp", a) * prior + coef("c1", a) * x1
                x2 = coef("d2", a) * f2 + coef("d1", a) * x1 + coef("d3", a) * end
                trial = [x0, x1, x2, end]
            else:
                trial = [coef("c0", a) * f0 + coef("cp", a) * prior + coef("c1", a) * end, end]
            for p in range(phases):
                diff[i, p, a, rows, :] = trial[p] - flux[i, p, a, rows, :]

    pair = [reduce(0), reduce(1)]
    yield
    solved = solve(jnp.concatenate(pair, axis=0), inverse)
    yield
    expand(0, solved[:dn])
    expand(1, solved[dn:])
    yield

    for i in range(2):
        o0, on = ends[i]
        mask = inside(origin + o0, on, total)
        rows = pl.ds(o0, on)
        for p in range(phases):
            for a in range(BLOCKS):
                middle = diff[i, p, a, rows, :]
                down = diff[i, p, a, pl.ds(o0 + 1, on), :]
                upper = diff[i, p, a, pl.ds(o0 - 1, on), :]
                sides = coef(("weight", p), a) * (down + upper)
                flux[i, p, a, rows, :] = (flux[i, p, a, rows, :] + coef(("centre", p), a) * middle + sides) * mask
    yield


def solve(right, inverse):
    count = right.shape[0]
    high, low = split(right)
    both = dot(jnp.concatenate([high, low], axis=0), inverse[0])
    return both[:count] + both[count:] + dot(high, inverse[1])


def wave_step(*arguments):
    for _ in step_stages(*arguments):
        pass


FINE_RATIO = FINE_STEP / (2.0 * FINE_SPACING)
COARSE_RATIO = COARSE_STEP / (2.0 * COARSE_SPACING)


def on_odd():
    return lax.rem(lax.axis_index("tile"), 2) == 1


def planes(phases):
    return [(c, p, a) for c in range(3) for p in range(phases) for a in range(BLOCKS)]


SPILL = ((0, 8), (8, 8), (16, 9))
SPILL_ROWS = 25
FAR_ROWS = 24 * 14
NEXT_ROWS = 24 * 6
SPARE = 8


def fetch(pairs, sems):
    copies = [pltpu.make_async_copy(source, target, sems.at[i]) for i, (source, target) in enumerate(pairs)]
    for copy in copies:
        copy.start()
    return copies


def at_tile(tile_rows, offset):
    return lax.axis_index("tile") * tile_rows - offset, lax.axis_size("tile") * tile_rows


def fine_kernel(
    x_hbm, fine_inverse_hbm, fine_table_hbm, coarse_inverse_hbm, coarse_table_hbm,
    wide_end, propagated, u_wide, u_far, u_near, coarse_inverse,
    x, matrix, fine_inverse, fine_table, coarse_table, sems,
    height, height_new, flux, diff, c_height, c_height_new, c_flux, c_diff,
):
    copies = fetch(
        (
            (x_hbm, x),
            (fine_table_hbm, fine_table),
            (coarse_table_hbm, coarse_table),
            (fine_inverse_hbm, fine_inverse),
            (coarse_inverse_hbm, coarse_inverse),
        ),
        sems,
    )
    for ref in (height, height_new, flux, diff):
        for edge in (pl.ds(0, 16), pl.ds(32, 16)):
            target = ref.at[..., edge, :]
            target[...] = jnp.zeros(target.shape, jnp.float32)
    for ref in (c_height, c_height_new, c_flux, c_diff):
        ref[...] = jnp.zeros(ref.shape, jnp.float32)
    row = lax.broadcasted_iota(jnp.int32, (512, 512), 0)
    column = lax.broadcasted_iota(jnp.int32, (512, 512), 1)
    chosen = column == (row & 3) * LANES + (row >> 2)
    matrix[...] = jnp.where(chosen, 1.0, 0.0).astype(jnp.bfloat16)
    copies[0].wait()

    parts = []
    for a in range(BLOCKS):
        for c in range(3):
            parts.append(x[c, :, a * 512 : (a + 1) * 512])
    phased = placed(jnp.concatenate(parts, axis=0), matrix[...])
    for c, p, a in planes(4):
        to = height.at[p, a] if c == 0 else flux.at[c - 1, p, a]
        base = (a * 3 + c) * ROWS
        to[16:32, :] = phased[base : base + ROWS, p * LANES : (p + 1) * LANES]

    def restricted(ref, p, a, first, count):
        total = None
        for q in (2 * p, 2 * p + 1):
            for r in (first, first + 1):
                part = ref(q, a)[pl.ds(r, count, stride=2), :]
                total = part if total is None else total + part
        return 0.25 * total

    for p in range(2):
        for a in range(BLOCKS):
            c_height[p, a, 12:20, :] = restricted(lambda q, b: height.at[q, b], p, a, 16, 8)
            for i in range(2):
                c_flux[i, p, a, 12:20, :] = restricted(lambda q, b: flux.at[i, q, b], p, a, 16, 8)
    for copy in copies[1:3]:
        copy.wait()

    coarse_arguments = (
        2, COARSE_NAMES, coarse_table, coarse_inverse, COARSE_RATIO, c_height, c_height_new, c_flux, c_diff,
        ((8, 16), (8, 16), ((8, 16), (8, 16))), *at_tile(ROWS // 2, 12),
    )
    fine_arguments = (4, FINE_NAMES, fine_table, fine_inverse, FINE_RATIO)
    place = at_tile(ROWS, 16)
    windows = ((12, 24), (12, 24), ((12, 24), (12, 24)))
    stages = (
        step_stages(*fine_arguments, height, height_new, flux, diff, windows, *place),
        step_stages(*coarse_arguments),
    )
    for _ in range(2):
        for stage in stages:
            next(stage)
    for copy in copies[3:]:
        copy.wait()
    for _ in zip(*stages):
        pass
    wave_step(*fine_arguments, height_new, height, flux, diff, ((12, 24), (8, 32), ((8, 32), (8, 32))), *place)
    wave_step(*fine_arguments, height, height_new, flux, diff, ((8, 32), (8, 32), ((8, 32), (4, 40))), *place)

    odd = on_odd()
    later = jnp.where(lax.axis_index("cuts") > 0, 1.0, 0.0).astype(jnp.float32)
    for n, (c, p, a) in enumerate(planes(2)):
        if c == 0:
            end = restricted(lambda q, b: height_new.at[q, b], p, a, 0, 24)
            step = c_height_new[p, a, 4:28, :]
        else:
            end = restricted(lambda q, b: flux.at[c - 1, q, b], p, a, 0, 24)
            step = c_flux[c - 1, p, a, 4:28, :]
        step = later * step
        propagated[c, p, a] = step[4:20]
        u = end - step
        u_wide[c, p, a] = u
        c_diff[0, p, a, 4:28, :] = u
        to_next = c_diff[0, p, a, 11:25, :]
        to_previous = c_diff[0, p, a, 7:21, :]
        u_far[n * 14 : n * 14 + 14, :] = jnp.where(odd, to_next, to_previous)
        u_near[n * 14 : n * 14 + 14, :] = jnp.where(odd, to_previous, to_next)
    for c, p, a in planes(4):
        source = height_new.at[p, a] if c == 0 else flux.at[c - 1, p, a]
        wide_end[c, p, a] = source[4:44, :]


def spill_kernel(wide_end, propagated, arrived, own, to_far, to_near, rows):
    del arrived
    odd = on_odd()
    for c, p, a in planes(2):
        value = propagated[c, p, a]
        rows[c, p, a, pl.ds(0, 16, stride=2), :] = value
        rows[c, p, a, pl.ds(1, 16, stride=2), :] = value
    for c, p, a in planes(4):
        start, count = SPILL[c]
        base = (p * BLOCKS + a) * SPILL_ROWS + start
        wide_end[c, p, a, 4:36, :] = wide_end[c, p, a, 4:36, :] - rows[c, p // 2, a]
        own[c, p, a] = wide_end[c, p, a, 12:28, :]
        to_next = wide_end[c, p, a, 28 : 28 + count, :]
        to_previous = wide_end[c, p, a, 12 - count : 12, :]
        to_far[base : base + count, :] = jnp.where(odd, to_next, to_previous)
        to_near[base : base + count, :] = jnp.where(odd, to_previous, to_next)


def join_kernel(own, near, out):
    odd = on_odd()

    @pl.when(odd)
    def _():
        for n in range(24):
            base = n * 14
            out[base + 6 : base + 14, :] = own[base + 6 : base + 14, :]
            out[base : base + 6, :] = own[base : base + 6, :] + near[base + 8 : base + 14, :]

    @pl.when(jnp.logical_not(odd))
    def _():
        for n in range(24):
            base = n * 14
            out[base : base + 8, :] = own[base : base + 8, :]
            out[base + 8 : base + 14, :] = own[base + 8 : base + 14, :] + near[base : base + 6, :]


def forward_kernel(far, out):
    odd = on_odd()
    for n in range(24):
        low = far[n * 14 : n * 14 + 6, :]
        high = far[n * 14 + 8 : n * 14 + 14, :]
        out[n * 6 : n * 6 + 6, :] = jnp.where(odd, low, high)


def assemble_kernel(own, far, near, out):
    odd = on_odd()
    for n, (c, p, a) in enumerate(planes(2)):
        to = out.at[c, p, a]
        distant = far[n * 14 : n * 14 + 14, :]
        close = near[n * 14 : n * 14 + 14, :]
        to[0:8, :] = jnp.zeros((8, LANES), jnp.float32)
        to[8:32, :] = own[c, p, a]
        to[32:40, :] = jnp.zeros((8, LANES), jnp.float32)
        to[7:21, :] = to[7:21, :] + jnp.where(odd, close, distant)
        to[19:33, :] = to[19:33, :] + jnp.where(odd, distant, close)


def first_kernel(assembled, cross, inverse, table, one, wide, height, height_new, flux, diff):
    odd = on_odd()

    @pl.when(lax.axis_index("cuts") < lax.axis_size("cuts") - 1)
    def _():
        for n, (c, p, a) in enumerate(planes(2)):
            to = height.at[p, a] if c == 0 else flux.at[c - 1, p, a]
            beyond = cross[n * 6 : n * 6 + 6, :]
            to[0:40, :] = assembled[c, p, a, 0:40, :]
            to[7:13, :] = to[7:13, :] + jnp.where(odd, beyond, 0.0)
            to[27:33, :] = to[27:33, :] + jnp.where(odd, 0.0, beyond)
        window = (8, 24)
        wave_step(
            2, COARSE_NAMES, table, inverse, COARSE_RATIO, height, height_new, flux, diff,
            (window, window, (window, window)), *at_tile(ROWS // 2, 16),
        )
        for c, p, a in planes(2):
            result = height_new.at[p, a] if c == 0 else flux.at[c - 1, p, a]
            one[c, p, a] = result[16:24, :]
            wide[c, p, a] = result[8:32, :]


def rest_kernel(wide, one, inverse, table, early, two, three, last, height, height_new, flux, diff):
    cut = lax.axis_index("cuts")
    arguments = (2, COARSE_NAMES, table, inverse, COARSE_RATIO)
    for c, p, a in planes(2):
        early[c, p, a] = one[c, p, a]
        last[c, p, a] = one[c, p, a]

    @pl.when(cut < 2)
    def _():
        for c, p, a in planes(2):
            to = height.at[p, a] if c == 0 else flux.at[c - 1, p, a]
            to[8:32, :] = wide[c, p, a]
        windows = ((8, 24), (12, 16), ((12, 16), (12, 16)))
        wave_step(*arguments, height, height_new, flux, diff, windows, *at_tile(ROWS // 2, 16))
        for c, p, a in planes(2):
            result = height_new.at[p, a] if c == 0 else flux.at[c - 1, p, a]
            two[c, p, a] = result[16:24, :]

    @pl.when(cut == 0)
    def _():
        windows = ((12, 16), (12, 16), ((16, 8), (16, 8)))
        wave_step(*arguments, height_new, height, flux, diff, windows, *at_tile(ROWS // 2, 16))
        for c, p, a in planes(2):
            result = height.at[p, a] if c == 0 else flux.at[c - 1, p, a]
            three[c, p, a] = result[16:24, :]


def natural_kernel(own, far, near, first, matrix, out, rows, total):
    odd = on_odd()
    for c, p, a in planes(2):
        rows[c, p, a, pl.ds(0, 8, stride=2), :] = first[c, p, a]
        rows[c, p, a, pl.ds(1, 8, stride=2), :] = first[c, p, a]
    for c, p, a in planes(4):
        start, count = SPILL[c]
        base = (p * BLOCKS + a) * SPILL_ROWS + start
        distant = far[base : base + count, :]
        close = near[base : base + count, :]
        to = total.at[c, p, a]
        to[0:ROWS, :] = own[c, p, a] + rows[c, p // 2, a]
        to[0:count, :] = to[0:count, :] + jnp.where(odd, close, distant)
        to[ROWS - count : ROWS, :] = to[ROWS - count : ROWS, :] + jnp.where(odd, distant, close)
    parts = []
    for a in range(BLOCKS):
        for c in range(3):
            parts.append(jnp.concatenate([total[c, p, a, 0:ROWS, :] for p in range(4)], axis=1))
    natural = placed(jnp.concatenate(parts, axis=0), matrix[...])
    for a in range(BLOCKS):
        for c in range(3):
            base = (a * 3 + c) * ROWS
            out[c, :, a * 512 : (a + 1) * 512] = natural[base : base + ROWS]


def final_kernel(base_end, second, third, fourth, matrix, out, rows, staged, sems):
    parts = []
    for a in range(BLOCKS):
        for c in range(3):
            pair = []
            for p in range(2):
                pair.append(second[c, p, a] + (third[c, p, a] + fourth[c, p, a]))
            parts.append(jnp.concatenate(pair, axis=1))
    spread = placed(jnp.concatenate(parts, axis=0), matrix[...])
    copies = []
    for a in range(BLOCKS):
        for c in range(3):
            base = (a * 3 + c) * 8
            for s in range(4):
                value = spread[base : base + 8, s * LANES : (s + 1) * LANES]
                rows[c, a * 4 + s, pl.ds(0, 8, stride=2), :] = value
                rows[c, a * 4 + s, pl.ds(1, 8, stride=2), :] = value
        for c in range(3):
            for s in range(4 * a, 4 * a + 4):
                cols = slice(s * LANES, (s + 1) * LANES)
                staged[c, :, cols] = base_end[c, :, cols] + rows[c, s]
        block = pl.ds(a * 512, 512)
        copies.append(pltpu.make_async_copy(staged.at[:, :, block], out.at[:, :, block], sems.at[a]))
        copies[-1].start()
    for copy in copies:
        copy.wait()


def f32(*shape):
    return jax.ShapeDtypeStruct(shape, jnp.float32)


def scratch(*shape):
    return pltpu.VMEM(shape, jnp.float32)


VMEM_SPEC = pl.BlockSpec(memory_space=pltpu.VMEM)
HBM_SPEC = pl.BlockSpec(memory_space=pltpu.HBM)


def in_hbm(array):
    return pltpu.with_memory_space_constraint(array, pltpu.HBM)


def call(kernel, ins, outs, scratches=(), name=None, cost=None):
    return pl.pallas_call(
        kernel,
        in_specs=[HBM_SPEC if own else VMEM_SPEC for own in ins],
        out_shape=[shape for shape, _ in outs],
        out_specs=[HBM_SPEC if own else VMEM_SPEC for _, own in outs],
        scratch_shapes=scratches,
        name=name,
        cost_estimate=cost,
        compiler_params=pltpu.CompilerParams(vmem_limit_bytes=VMEM_LIMIT),
    )


def per_device(start_states):
    tiles = lax.axis_size("tile")
    far_pairs = [(i, j) for k in range(1, tiles - 1, 2) for i, j in ((k, k + 1), (k + 1, k))]
    near_pairs = [(i, i ^ 1) for i in range(tiles)]
    dma = pltpu.SemaphoreType.DMA

    def bf16(array):
        return jax.ShapeDtypeStruct(array.shape, jnp.bfloat16)

    def here(array):
        return pltpu.VMEM(array.shape, array.dtype)

    coarse = (f32(3, 2, BLOCKS, 8, LANES), False)
    spilt = (f32(16 * SPILL_ROWS + SPARE, LANES), False)
    far_rows = (f32(FAR_ROWS + SPARE, LANES), False)
    last_rows = (f32(NEXT_ROWS + SPARE, LANES), False)
    fetched = (start_states[0], FINE_INVERSE, FINE_TABLE, COARSE_INVERSE, COARSE_TABLE)
    wide_end, propagated, u_wide, u_far, u_near, coarse_inverse = call(
        fine_kernel,
        [True] * 5,
        [
            (f32(3, 4, BLOCKS, 40, LANES), False),
            (f32(3, 2, BLOCKS, 16, LANES), False),
            (f32(3, 2, BLOCKS, 24, LANES), False),
            far_rows,
            far_rows,
            (bf16(COARSE_INVERSE), False),
        ],
        [
            scratch(3, ROWS, NX),
            pltpu.VMEM((512, 512), jnp.bfloat16),
            here(FINE_INVERSE),
            here(FINE_TABLE),
            here(COARSE_TABLE),
            dma((5,)),
            scratch(4, BLOCKS, 48, LANES),
            scratch(4, BLOCKS, 48, LANES),
            scratch(2, 4, BLOCKS, 48, LANES),
            scratch(2, 4, BLOCKS, 48, LANES),
            scratch(2, BLOCKS, 32, LANES),
            scratch(2, BLOCKS, 32, LANES),
            scratch(2, 2, BLOCKS, 32, LANES),
            scratch(2, 2, BLOCKS, 32, LANES),
        ],
        name="fine",
    )(*[in_hbm(array) for array in fetched])
    senders = range(lax.axis_size("cuts") - 1)

    def of_senders(pairs):
        return [(k * tiles + i, k * tiles + j) for k in senders for i, j in pairs]

    u_near = lax.ppermute(u_near, "tile", near_pairs)
    (u_far,) = call(join_kernel, [False] * 2, [far_rows], name="join")(u_far, u_near)
    own, spill_far, spill_near = call(
        spill_kernel,
        [False] * 3,
        [(f32(3, 4, BLOCKS, ROWS, LANES), False), spilt, spilt],
        [scratch(3, 2, BLOCKS, 32, LANES)],
        name="spill",
    )(wide_end, propagated, u_far)
    u_far = lax.ppermute(u_far, ("cuts", "tile"), of_senders(far_pairs))
    spill_far = lax.ppermute(spill_far, "tile", far_pairs)
    spill_near = lax.ppermute(spill_near, "tile", near_pairs)
    (cross,) = call(forward_kernel, [False], [last_rows], name="forward")(u_far)
    cross = lax.ppermute(cross, "tile", near_pairs)

    state = [
        scratch(2, BLOCKS, 48, LANES),
        scratch(2, BLOCKS, 48, LANES),
        scratch(2, 2, BLOCKS, 48, LANES),
        scratch(2, 2, BLOCKS, 48, LANES),
    ]
    (assembled,) = call(
        assemble_kernel,
        [False] * 3,
        [(f32(3, 2, BLOCKS, 48, LANES), False)],
        name="assemble",
        cost=pl.CostEstimate(flops=COST, bytes_accessed=COST // 100, transcendentals=0),
    )(u_wide, u_far, u_near)
    one, wide = call(
        first_kernel, [False] * 4, [coarse, (f32(3, 2, BLOCKS, 24, LANES), False)], state, name="first"
    )(assembled, cross, coarse_inverse, COARSE_TABLE)
    early, two, three, last = call(rest_kernel, [False] * 4, [coarse] * 4, state, name="rest")(
        wide, one, coarse_inverse, COARSE_TABLE
    )
    first = lax.ppermute(early, "cuts", [(0, 1), (1, 2)])
    second = lax.ppermute(two, "cuts", [(0, 2), (1, 3)])
    third = lax.ppermute(three, "cuts", [(0, 3)])
    fourth = lax.ppermute(last, "cuts", [(2, 3)])
    (natural,) = call(
        natural_kernel,
        [False] * 5,
        [(f32(3, ROWS, NX), False)],
        [scratch(3, 2, BLOCKS, ROWS, LANES), scratch(3, 4, BLOCKS, ROWS + SPARE, LANES)],
        name="natural",
    )(own, spill_far, spill_near, first, NATURAL)
    (out,) = call(
        final_kernel,
        [False] * 5,
        [(f32(3, ROWS, NX), True)],
        [scratch(3, 16, ROWS, LANES), scratch(3, ROWS, NX), dma((BLOCKS,))],
        name="final",
    )(natural, third, second, fourth, SPREAD)
    return out[None]


def solution(mesh):
    spec = P("cuts", None, "tile", None)
    return jax.shard_map(per_device, mesh=mesh, in_specs=(spec,), out_specs=spec, check_vma=False)
```

```python
import jax
import jax.numpy as jnp
import ml_dtypes
import numpy as np
from jax import lax
from jax.experimental import pallas as pl
from jax.experimental.pallas import tpu as pltpu
from jax.sharding import PartitionSpec as P

STEPS = 3
FINE_SPACING = 0.05
COARSE_SPACING = 0.1
FINE_STEP = 0.015
COARSE_STEP = 0.045

NX = 2048
ROWS = 16
UNKNOWNS = 512
BLOCKS = 4
LANES = 128
COST = 10**10
VMEM_LIMIT = 48 * 1024 * 1024


def halves(values):
    high = values.astype(np.float32).astype(ml_dtypes.bfloat16)
    low = (values - high.astype(np.float64)).astype(np.float32).astype(ml_dtypes.bfloat16)
    return high, low


def shifted(values):
    return np.concatenate([[0.0], values[:-1]])


def eliminated(lower, middle, upper):
    lower_e, lower_o = lower[0::2], lower[1::2]
    middle_e, middle_o = middle[0::2], middle[1::2]
    upper_e, upper_o = upper[0::2], upper[1::2]
    middle_n = np.append(middle_e[1:], 1.0)
    lower_n = np.append(lower_e[1:], 0.0)
    upper_n = np.append(upper_e[1:], 0.0)
    alpha = -lower_o / middle_e
    gamma = -upper_o / middle_n
    reduced = (alpha * lower_e, middle_o + alpha * upper_e + gamma * lower_n, gamma * upper_n)
    return alpha, gamma, reduced


def operator_tables(phases, columns, spacing, time_step):
    stride = NX // columns
    centers = (np.arange(columns) + 0.5) * stride
    depth = 0.9 + 0.3 * np.sin(6.0 * np.pi * centers / NX)
    beta = depth * depth / 3.0
    coupling = beta / (spacing * spacing)
    lower = -coupling.copy()
    lower[0] = 0.0
    upper = -coupling.copy()
    upper[-1] = 0.0
    middle = 1.0 + 2.0 * coupling
    slope = time_step * depth / (2.0 * spacing)
    weight = beta / (spacing * spacing + 4.0 * beta)
    rows = {}
    for p in range(phases):
        rows["slope", p] = slope[p::phases]
        rows["weight", p] = weight[p::phases]
        rows["centre", p] = 1.0 - 2.0 * weight[p::phases]
    alpha, gamma, first = eliminated(lower, middle, upper)
    if phases == 4:
        alpha2, gamma2, last = eliminated(*first)
        a1, a3, g1, g3 = alpha[0::2], alpha[1::2], gamma[0::2], gamma[1::2]
        rows["s0"] = alpha2 * a1
        rows["s1"] = alpha2
        rows["s2"] = a3 + alpha2 * g1
        rows["n1"] = shifted(gamma2)
        rows["n0"] = shifted(gamma2) * a1 + shifted(g3)
        rows["n2"] = shifted(gamma2) * g1
        l1, m1, u1 = (v[0::2] for v in first)
        rows["b1"] = 1.0 / m1
        rows["b0"] = a1 / m1
        rows["b2"] = g1 / m1
        rows["bp"] = -l1 / m1
        rows["b3"] = -u1 / m1
        rows["c0"] = 1.0 / middle[0::4]
        rows["cp"] = -lower[0::4] / middle[0::4]
        rows["c1"] = -upper[0::4] / middle[0::4]
        rows["d2"] = 1.0 / middle[2::4]
        rows["d1"] = -lower[2::4] / middle[2::4]
        rows["d3"] = -upper[2::4] / middle[2::4]
    else:
        last = first
        rows["s0"] = alpha
        rows["n0"] = shifted(gamma)
        rows["c0"] = 1.0 / middle[0::2]
        rows["cp"] = -lower[0::2] / middle[0::2]
        rows["c1"] = -upper[0::2] / middle[0::2]
    low, mid, up = last
    matrix = np.diag(mid) + np.diag(low[1:], -1) + np.diag(up[:-1], 1)
    inverse = np.linalg.inv(matrix)
    names = {name: i for i, name in enumerate(rows)}
    table = np.stack(list(rows.values())).reshape(-1, LANES).astype(np.float32)
    return names, table, np.stack(halves(inverse.T))


FINE_NAMES, FINE_TABLE, FINE_INVERSE = operator_tables(4, NX, FINE_SPACING, FINE_STEP)
COARSE_NAMES, COARSE_TABLE, COARSE_INVERSE = operator_tables(2, NX // 2, COARSE_SPACING, COARSE_STEP)


def phase_matrix():
    matrix = np.zeros((512, 512), np.float32)
    j = np.arange(512)
    matrix[j, (j % 4) * LANES + j // 4] = 1.0
    return matrix


NATURAL = phase_matrix().T.copy().astype(ml_dtypes.bfloat16)


def spread_matrix():
    matrix = np.zeros((256, 512), np.float32)
    c = np.arange(512)
    coarse = c // 2
    matrix[(coarse % 2) * LANES + coarse // 2, c] = 1.0
    return matrix


SPREAD = spread_matrix().astype(ml_dtypes.bfloat16)


def split(values):
    high = values.astype(jnp.bfloat16)
    low = (values - high.astype(jnp.float32)).astype(jnp.bfloat16)
    return high, low


def dot(a, b):
    return jnp.dot(a, b, preferred_element_type=jnp.float32)


def placed(values, matrix):
    count = values.shape[0]
    high, low = split(values)
    both = dot(jnp.concatenate([high, low], axis=0), matrix)
    return both[:count] + both[count:]


def lane_index(rows):
    return lax.broadcasted_iota(jnp.int32, (rows, LANES), 1)


def following(tiles):
    lane = lane_index(tiles[0].shape[0])
    rolled = [pltpu.roll(t, LANES - 1, 1) for t in tiles] + [jnp.zeros_like(tiles[0])]
    return [jnp.where(lane == LANES - 1, rolled[a + 1], rolled[a]) for a in range(BLOCKS)]


def preceding(tiles):
    lane = lane_index(tiles[0].shape[0])
    rolled = [jnp.zeros_like(tiles[0])] + [pltpu.roll(t, 1, 1) for t in tiles]
    return [jnp.where(lane == 0, rolled[a], rolled[a + 1]) for a in range(BLOCKS)]


def inside(first, count, total):
    row = lax.broadcasted_iota(jnp.int32, (count, LANES), 0) + first
    return jnp.where((row >= 0) & (row < total), 1.0, 0.0).astype(jnp.float32)


def step_stages(phases, names, table, inverse, ratio, height, height_new, flux, diff, windows, origin, total):
    (h0, hn), (d0, dn), ends = windows
    last = phases - 1

    def coef(name, a):
        i = names[name] * BLOCKS + a
        return table[i : i + 1, :]

    mask = inside(origin + h0, hn, total)
    rows = pl.ds(h0, hn)
    before = preceding([flux[0, last, a, rows, :] for a in range(BLOCKS)])
    after = following([flux[0, 0, a, rows, :] for a in range(BLOCKS)])
    for p in range(phases):
        for a in range(BLOCKS):
            right = after[a] if p == last else flux[0, p + 1, a, rows, :]
            left = before[a] if p == 0 else flux[0, p - 1, a, rows, :]
            down = flux[1, p, a, pl.ds(h0 + 1, hn), :]
            upper = flux[1, p, a, pl.ds(h0 - 1, hn), :]
            change = (right - left) + (down - upper)
            height_new[p, a, rows, :] = (height[p, a, rows, :] - ratio * change) * mask
    yield

    rows = pl.ds(d0, dn)
    mask = inside(origin + d0, dn, total)

    def reduce(i):
        if i == 0:
            before = preceding([height_new[last, a, rows, :] for a in range(BLOCKS)])
            after = following([height_new[0, a, rows, :] for a in range(BLOCKS)])
        own, passed = [], []
        for a in range(BLOCKS):
            force = []
            for p in range(phases):
                if i == 0:
                    right = after[a] if p == last else height_new[p + 1, a, rows, :]
                    left = before[a] if p == 0 else height_new[p - 1, a, rows, :]
                    value = flux[0, p, a, rows, :] - coef(("slope", p), a) * (right - left)
                else:
                    down = height_new[p, a, pl.ds(d0 + 1, dn), :]
                    upper = height_new[p, a, pl.ds(d0 - 1, dn), :]
                    value = (flux[1, p, a, rows, :] - coef(("slope", p), a) * (down - upper)) * mask
                if p < last:
                    diff[i, p, a, rows, :] = value
                force.append(value)
            kept = force[last] + coef("s0", a) * force[0]
            sent = coef("n0", a) * force[0]
            if phases == 4:
                kept = kept + coef("s1", a) * force[1] + coef("s2", a) * force[2]
                sent = sent + coef("n1", a) * force[1] + coef("n2", a) * force[2]
            own.append(kept)
            passed.append(sent)
        arrived = following(passed)
        return jnp.concatenate([own[a] + arrived[a] for a in range(BLOCKS)], axis=1)

    def expand(i, solved):
        ends = [solved[:, a * LANES : (a + 1) * LANES] for a in range(BLOCKS)]
        before = preceding(ends)
        for a in range(BLOCKS):
            end, prior = ends[a], before[a]
            f0 = diff[i, 0, a, rows, :]
            if phases == 4:
                f1 = diff[i, 1, a, rows, :]
                f2 = diff[i, 2, a, rows, :]
                x1 = (
                    coef("b1", a) * f1
                    + coef("b0", a) * f0
                    + coef("b2", a) * f2
                    + coef("bp", a) * prior
                    + coef("b3", a) * end
                )
                x0 = coef("c0", a) * f0 + coef("cp", a) * prior + coef("c1", a) * x1
                x2 = coef("d2", a) * f2 + coef("d1", a) * x1 + coef("d3", a) * end
                trial = [x0, x1, x2, end]
            else:
                trial = [coef("c0", a) * f0 + coef("cp", a) * prior + coef("c1", a) * end, end]
            for p in range(phases):
                diff[i, p, a, rows, :] = trial[p] - flux[i, p, a, rows, :]

    pair = [reduce(0), reduce(1)]
    yield
    solved = solve(jnp.concatenate(pair, axis=0), inverse)
    yield
    expand(0, solved[:dn])
    expand(1, solved[dn:])
    yield

    for i in range(2):
        o0, on = ends[i]
        mask = inside(origin + o0, on, total)
        rows = pl.ds(o0, on)
        for p in range(phases):
            for a in range(BLOCKS):
                middle = diff[i, p, a, rows, :]
                down = diff[i, p, a, pl.ds(o0 + 1, on), :]
                upper = diff[i, p, a, pl.ds(o0 - 1, on), :]
                sides = coef(("weight", p), a) * (down + upper)
                flux[i, p, a, rows, :] = (flux[i, p, a, rows, :] + coef(("centre", p), a) * middle + sides) * mask
    yield


def solve(right, inverse):
    count = right.shape[0]
    high, low = split(right)
    both = dot(jnp.concatenate([high, low], axis=0), inverse[0])
    return both[:count] + both[count:] + dot(high, inverse[1])


def wave_step(*arguments):
    for _ in step_stages(*arguments):
        pass


FINE_RATIO = FINE_STEP / (2.0 * FINE_SPACING)
COARSE_RATIO = COARSE_STEP / (2.0 * COARSE_SPACING)


def on_odd():
    return lax.rem(lax.axis_index("tile"), 2) == 1


def planes(phases):
    return [(c, p, a) for c in range(3) for p in range(phases) for a in range(BLOCKS)]


SPILL = ((0, 8), (8, 8), (16, 9))
SPILL_ROWS = 25
FAR_ROWS = 24 * 14
NEXT_ROWS = 24 * 6
SPARE = 8


def fetch(pairs, sems):
    copies = [pltpu.make_async_copy(source, target, sems.at[i]) for i, (source, target) in enumerate(pairs)]
    for copy in copies:
        copy.start()
    return copies


def at_tile(tile_rows, offset):
    return lax.axis_index("tile") * tile_rows - offset, lax.axis_size("tile") * tile_rows


def fine_kernel(
    x_hbm, fine_inverse_hbm, fine_table_hbm, coarse_inverse_hbm, coarse_table_hbm,
    wide_end, propagated, u_wide, u_far, u_near, coarse_inverse,
    x, matrix, fine_inverse, fine_table, coarse_table, sems,
    height, height_new, flux, diff, c_height, c_height_new, c_flux, c_diff,
):
    copies = fetch(
        (
            (x_hbm, x),
            (fine_table_hbm, fine_table),
            (coarse_table_hbm, coarse_table),
            (fine_inverse_hbm, fine_inverse),
            (coarse_inverse_hbm, coarse_inverse),
        ),
        sems,
    )
    for ref in (height, height_new, flux, diff):
        for edge in (pl.ds(0, 16), pl.ds(32, 16)):
            target = ref.at[..., edge, :]
            target[...] = jnp.zeros(target.shape, jnp.float32)
    for ref in (c_height, c_height_new, c_flux, c_diff):
        ref[...] = jnp.zeros(ref.shape, jnp.float32)
    row = lax.broadcasted_iota(jnp.int32, (512, 512), 0)
    column = lax.broadcasted_iota(jnp.int32, (512, 512), 1)
    chosen = column == (row & 3) * LANES + (row >> 2)
    matrix[...] = jnp.where(chosen, 1.0, 0.0).astype(jnp.bfloat16)
    copies[0].wait()

    parts = []
    for a in range(BLOCKS):
        for c in range(3):
            parts.append(x[c, :, a * 512 : (a + 1) * 512])
    phased = placed(jnp.concatenate(parts, axis=0), matrix[...])
    for c, p, a in planes(4):
        to = height.at[p, a] if c == 0 else flux.at[c - 1, p, a]
        base = (a * 3 + c) * ROWS
        to[16:32, :] = phased[base : base + ROWS, p * LANES : (p + 1) * LANES]

    def restricted(ref, p, a, first, count):
        total = None
        for q in (2 * p, 2 * p + 1):
            for r in (first, first + 1):
                part = ref(q, a)[pl.ds(r, count, stride=2), :]
                total = part if total is None else total + part
        return 0.25 * total

    for p in range(2):
        for a in range(BLOCKS):
            c_height[p, a, 12:20, :] = restricted(lambda q, b: height.at[q, b], p, a, 16, 8)
            for i in range(2):
                c_flux[i, p, a, 12:20, :] = restricted(lambda q, b: flux.at[i, q, b], p, a, 16, 8)
    for copy in copies[1:3]:
        copy.wait()

    coarse_arguments = (
        2, COARSE_NAMES, coarse_table, coarse_inverse, COARSE_RATIO, c_height, c_height_new, c_flux, c_diff,
        ((8, 16), (8, 16), ((8, 16), (8, 16))), *at_tile(ROWS // 2, 12),
    )
    fine_arguments = (4, FINE_NAMES, fine_table, fine_inverse, FINE_RATIO)
    place = at_tile(ROWS, 16)
    windows = ((12, 24), (12, 24), ((12, 24), (12, 24)))
    stages = (
        step_stages(*fine_arguments, height, height_new, flux, diff, windows, *place),
        step_stages(*coarse_arguments),
    )
    for _ in range(2):
        for stage in stages:
            next(stage)
    for copy in copies[3:]:
        copy.wait()
    for _ in zip(*stages):
        pass
    wave_step(*fine_arguments, height_new, height, flux, diff, ((12, 24), (8, 32), ((8, 32), (8, 32))), *place)
    wave_step(*fine_arguments, height, height_new, flux, diff, ((8, 32), (8, 32), ((8, 32), (4, 40))), *place)

    odd = on_odd()
    later = jnp.where(lax.axis_index("cuts") > 0, 1.0, 0.0).astype(jnp.float32)
    for n, (c, p, a) in enumerate(planes(2)):
        if c == 0:
            end = restricted(lambda q, b: height_new.at[q, b], p, a, 0, 24)
            step = c_height_new[p, a, 4:28, :]
        else:
            end = restricted(lambda q, b: flux.at[c - 1, q, b], p, a, 0, 24)
            step = c_flux[c - 1, p, a, 4:28, :]
        step = later * step
        propagated[c, p, a] = step[4:20]
        u = end - step
        u_wide[c, p, a] = u
        c_diff[0, p, a, 4:28, :] = u
        to_next = c_diff[0, p, a, 11:25, :]
        to_previous = c_diff[0, p, a, 7:21, :]
        u_far[n * 14 : n * 14 + 14, :] = jnp.where(odd, to_next, to_previous)
        u_near[n * 14 : n * 14 + 14, :] = jnp.where(odd, to_previous, to_next)
    for c, p, a in planes(4):
        source = height_new.at[p, a] if c == 0 else flux.at[c - 1, p, a]
        wide_end[c, p, a] = source[4:44, :]


def spill_kernel(wide_end, propagated, arrived, own, to_far, to_near, rows, total):
    del arrived
    odd = on_odd()
    for c, p, a in planes(2):
        value = propagated[c, p, a]
        rows[c, p, a, pl.ds(0, 16, stride=2), :] = value
        rows[c, p, a, pl.ds(1, 16, stride=2), :] = value
    for c, p, a in planes(4):
        start, count = SPILL[c]
        base = (p * BLOCKS + a) * SPILL_ROWS + start
        to = total.at[c, p, a]
        to[0:40, :] = wide_end[c, p, a]
        to[4:36, :] = to[4:36, :] - rows[c, p // 2, a]
        own[c, p, a] = to[12:28, :]
        to_next = to[28 : 28 + count, :]
        to_previous = to[12 - count : 12, :]
        to_far[base : base + count, :] = jnp.where(odd, to_next, to_previous)
        to_near[base : base + count, :] = jnp.where(odd, to_previous, to_next)


def join_kernel(own, near, out):
    odd = on_odd()

    @pl.when(odd)
    def _():
        for n in range(24):
            base = n * 14
            out[base + 6 : base + 14, :] = own[base + 6 : base + 14, :]
            out[base : base + 6, :] = own[base : base + 6, :] + near[base + 8 : base + 14, :]

    @pl.when(jnp.logical_not(odd))
    def _():
        for n in range(24):
            base = n * 14
            out[base : base + 8, :] = own[base : base + 8, :]
            out[base + 8 : base + 14, :] = own[base + 8 : base + 14, :] + near[base : base + 6, :]


def forward_kernel(far, out):
    odd = on_odd()
    for n in range(24):
        low = far[n * 14 : n * 14 + 6, :]
        high = far[n * 14 + 8 : n * 14 + 14, :]
        out[n * 6 : n * 6 + 6, :] = jnp.where(odd, low, high)


def assemble_kernel(own, far, near, out):
    odd = on_odd()
    for n, (c, p, a) in enumerate(planes(2)):
        to = out.at[c, p, a]
        distant = far[n * 14 : n * 14 + 14, :]
        close = near[n * 14 : n * 14 + 14, :]
        to[0:8, :] = jnp.zeros((8, LANES), jnp.float32)
        to[8:32, :] = own[c, p, a]
        to[32:40, :] = jnp.zeros((8, LANES), jnp.float32)
        to[7:21, :] = to[7:21, :] + jnp.where(odd, close, distant)
        to[19:33, :] = to[19:33, :] + jnp.where(odd, distant, close)


def first_kernel(assembled, cross, inverse, table, one, wide, height, height_new, flux, diff):
    odd = on_odd()

    @pl.when(lax.axis_index("cuts") < lax.axis_size("cuts") - 1)
    def _():
        for n, (c, p, a) in enumerate(planes(2)):
            to = height.at[p, a] if c == 0 else flux.at[c - 1, p, a]
            beyond = cross[n * 6 : n * 6 + 6, :]
            to[0:40, :] = assembled[c, p, a, 0:40, :]
            to[7:13, :] = to[7:13, :] + jnp.where(odd, beyond, 0.0)
            to[27:33, :] = to[27:33, :] + jnp.where(odd, 0.0, beyond)
        window = (8, 24)
        wave_step(
            2, COARSE_NAMES, table, inverse, COARSE_RATIO, height, height_new, flux, diff,
            (window, window, (window, window)), *at_tile(ROWS // 2, 16),
        )
        for c, p, a in planes(2):
            result = height_new.at[p, a] if c == 0 else flux.at[c - 1, p, a]
            one[c, p, a] = result[16:24, :]
            wide[c, p, a] = result[8:32, :]


def rest_kernel(wide, one, inverse, table, early, two, three, last, height, height_new, flux, diff):
    cut = lax.axis_index("cuts")
    arguments = (2, COARSE_NAMES, table, inverse, COARSE_RATIO)
    for c, p, a in planes(2):
        early[c, p, a] = one[c, p, a]
        last[c, p, a] = one[c, p, a]

    @pl.when(cut < 2)
    def _():
        for c, p, a in planes(2):
            to = height.at[p, a] if c == 0 else flux.at[c - 1, p, a]
            to[8:32, :] = wide[c, p, a]
        windows = ((8, 24), (12, 16), ((12, 16), (12, 16)))
        wave_step(*arguments, height, height_new, flux, diff, windows, *at_tile(ROWS // 2, 16))
        for c, p, a in planes(2):
            result = height_new.at[p, a] if c == 0 else flux.at[c - 1, p, a]
            two[c, p, a] = result[16:24, :]

    @pl.when(cut == 0)
    def _():
        windows = ((12, 16), (12, 16), ((16, 8), (16, 8)))
        wave_step(*arguments, height_new, height, flux, diff, windows, *at_tile(ROWS // 2, 16))
        for c, p, a in planes(2):
            result = height.at[p, a] if c == 0 else flux.at[c - 1, p, a]
            three[c, p, a] = result[16:24, :]


def natural_kernel(own, far, near, first, matrix, out, rows, total):
    odd = on_odd()
    for c, p, a in planes(2):
        rows[c, p, a, pl.ds(0, 8, stride=2), :] = first[c, p, a]
        rows[c, p, a, pl.ds(1, 8, stride=2), :] = first[c, p, a]
    for c, p, a in planes(4):
        start, count = SPILL[c]
        base = (p * BLOCKS + a) * SPILL_ROWS + start
        distant = far[base : base + count, :]
        close = near[base : base + count, :]
        to = total.at[c, p, a]
        to[0:ROWS, :] = own[c, p, a] + rows[c, p // 2, a]
        to[0:count, :] = to[0:count, :] + jnp.where(odd, close, distant)
        to[ROWS - count : ROWS, :] = to[ROWS - count : ROWS, :] + jnp.where(odd, distant, close)
    parts = []
    for a in range(BLOCKS):
        for c in range(3):
            parts.append(jnp.concatenate([total[c, p, a, 0:ROWS, :] for p in range(4)], axis=1))
    natural = placed(jnp.concatenate(parts, axis=0), matrix[...])
    for a in range(BLOCKS):
        for c in range(3):
            base = (a * 3 + c) * ROWS
            out[c, :, a * 512 : (a + 1) * 512] = natural[base : base + ROWS]


def final_kernel(base_end, second, third, fourth, matrix, out, rows, staged, sems):
    parts = []
    for a in range(BLOCKS):
        for c in range(3):
            pair = []
            for p in range(2):
                pair.append(second[c, p, a] + (third[c, p, a] + fourth[c, p, a]))
            parts.append(jnp.concatenate(pair, axis=1))
    spread = placed(jnp.concatenate(parts, axis=0), matrix[...])
    copies = []
    for a in range(BLOCKS):
        for c in range(3):
            base = (a * 3 + c) * 8
            for s in range(4):
                value = spread[base : base + 8, s * LANES : (s + 1) * LANES]
                rows[c, a * 4 + s, pl.ds(0, 8, stride=2), :] = value
                rows[c, a * 4 + s, pl.ds(1, 8, stride=2), :] = value
        for c in range(3):
            for s in range(4 * a, 4 * a + 4):
                cols = slice(s * LANES, (s + 1) * LANES)
                staged[c, :, cols] = base_end[c, :, cols] + rows[c, s]
        block = pl.ds(a * 512, 512)
        copies.append(pltpu.make_async_copy(staged.at[:, :, block], out.at[:, :, block], sems.at[a]))
        copies[-1].start()
    for copy in copies:
        copy.wait()


def f32(*shape):
    return jax.ShapeDtypeStruct(shape, jnp.float32)


def scratch(*shape):
    return pltpu.VMEM(shape, jnp.float32)


VMEM_SPEC = pl.BlockSpec(memory_space=pltpu.VMEM)
HBM_SPEC = pl.BlockSpec(memory_space=pltpu.HBM)


def in_hbm(array):
    return pltpu.with_memory_space_constraint(array, pltpu.HBM)


def call(kernel, ins, outs, scratches=(), name=None, cost=None):
    return pl.pallas_call(
        kernel,
        in_specs=[HBM_SPEC if own else VMEM_SPEC for own in ins],
        out_shape=[shape for shape, _ in outs],
        out_specs=[HBM_SPEC if own else VMEM_SPEC for _, own in outs],
        scratch_shapes=scratches,
        name=name,
        cost_estimate=cost,
        compiler_params=pltpu.CompilerParams(vmem_limit_bytes=VMEM_LIMIT),
    )


def per_device(start_states):
    tiles = lax.axis_size("tile")
    far_pairs = [(i, j) for k in range(1, tiles - 1, 2) for i, j in ((k, k + 1), (k + 1, k))]
    near_pairs = [(i, i ^ 1) for i in range(tiles)]
    dma = pltpu.SemaphoreType.DMA

    def bf16(array):
        return jax.ShapeDtypeStruct(array.shape, jnp.bfloat16)

    def here(array):
        return pltpu.VMEM(array.shape, array.dtype)

    coarse = (f32(3, 2, BLOCKS, 8, LANES), False)
    spilt = (f32(16 * SPILL_ROWS + SPARE, LANES), False)
    far_rows = (f32(FAR_ROWS + SPARE, LANES), False)
    last_rows = (f32(NEXT_ROWS + SPARE, LANES), False)
    fetched = (start_states[0], FINE_INVERSE, FINE_TABLE, COARSE_INVERSE, COARSE_TABLE)
    wide_end, propagated, u_wide, u_far, u_near, coarse_inverse = call(
        fine_kernel,
        [True] * 5,
        [
            (f32(3, 4, BLOCKS, 40, LANES), False),
            (f32(3, 2, BLOCKS, 16, LANES), False),
            (f32(3, 2, BLOCKS, 24, LANES), False),
            far_rows,
            far_rows,
            (bf16(COARSE_INVERSE), False),
        ],
        [
            scratch(3, ROWS, NX),
            pltpu.VMEM((512, 512), jnp.bfloat16),
            here(FINE_INVERSE),
            here(FINE_TABLE),
            here(COARSE_TABLE),
            dma((5,)),
            scratch(4, BLOCKS, 48, LANES),
            scratch(4, BLOCKS, 48, LANES),
            scratch(2, 4, BLOCKS, 48, LANES),
            scratch(2, 4, BLOCKS, 48, LANES),
            scratch(2, BLOCKS, 32, LANES),
            scratch(2, BLOCKS, 32, LANES),
            scratch(2, 2, BLOCKS, 32, LANES),
            scratch(2, 2, BLOCKS, 32, LANES),
        ],
        name="fine",
    )(*[in_hbm(array) for array in fetched])
    senders = range(lax.axis_size("cuts") - 1)

    def of_senders(pairs):
        return [(k * tiles + i, k * tiles + j) for k in senders for i, j in pairs]

    u_near = lax.ppermute(u_near, "tile", near_pairs)
    (u_far,) = call(join_kernel, [False] * 2, [far_rows], name="join")(u_far, u_near)
    own, spill_far, spill_near = call(
        spill_kernel,
        [False] * 3,
        [(f32(3, 4, BLOCKS, ROWS, LANES), False), spilt, spilt],
        [scratch(3, 2, BLOCKS, 32, LANES), scratch(3, 4, BLOCKS, 48, LANES)],
        name="spill",
    )(wide_end, propagated, u_far)
    u_far = lax.ppermute(u_far, ("cuts", "tile"), of_senders(far_pairs))
    spill_far = lax.ppermute(spill_far, "tile", far_pairs)
    spill_near = lax.ppermute(spill_near, "tile", near_pairs)
    (cross,) = call(forward_kernel, [False], [last_rows], name="forward")(u_far)
    cross = lax.ppermute(cross, "tile", near_pairs)

    state = [
        scratch(2, BLOCKS, 48, LANES),
        scratch(2, BLOCKS, 48, LANES),
        scratch(2, 2, BLOCKS, 48, LANES),
        scratch(2, 2, BLOCKS, 48, LANES),
    ]
    (assembled,) = call(
        assemble_kernel,
        [False] * 3,
        [(f32(3, 2, BLOCKS, 48, LANES), False)],
        name="assemble",
        cost=pl.CostEstimate(flops=COST, bytes_accessed=COST // 100, transcendentals=0),
    )(u_wide, u_far, u_near)
    one, wide = call(
        first_kernel, [False] * 4, [coarse, (f32(3, 2, BLOCKS, 24, LANES), False)], state, name="first"
    )(assembled, cross, coarse_inverse, COARSE_TABLE)
    early, two, three, last = call(rest_kernel, [False] * 4, [coarse] * 4, state, name="rest")(
        wide, one, coarse_inverse, COARSE_TABLE
    )
    first = lax.ppermute(early, "cuts", [(0, 1), (1, 2)])
    second = lax.ppermute(two, "cuts", [(0, 2), (1, 3)])
    third = lax.ppermute(three, "cuts", [(0, 3)])
    fourth = lax.ppermute(last, "cuts", [(2, 3)])
    (natural,) = call(
        natural_kernel,
        [False] * 5,
        [(f32(3, ROWS, NX), False)],
        [scratch(3, 2, BLOCKS, ROWS, LANES), scratch(3, 4, BLOCKS, ROWS + SPARE, LANES)],
        name="natural",
    )(own, spill_far, spill_near, first, NATURAL)
    (out,) = call(
        final_kernel,
        [False] * 5,
        [(f32(3, ROWS, NX), True)],
        [scratch(3, 16, ROWS, LANES), scratch(3, ROWS, NX), dma((BLOCKS,))],
        name="final",
    )(natural, third, second, fourth, SPREAD)
    return out[None]


def solution(mesh):
    spec = P("cuts", None, "tile", None)
    return jax.shard_map(per_device, mesh=mesh, in_specs=(spec,), out_specs=spec, check_vma=False)
```
